512 devices in a mesh: wide: 64 (over x, z, core), narrow: 8 (over y).
Axes of the slice: x: 4, y: 8, z: 8, core: 2. Of those that a mesh axis runs over, the one named last changes fastest.
Arguments:
- positions: float32 [3, 131072], P(None, ('wide', 'narrow')), may hold values from -6 to 6
- velocities: float32 [3, 131072], P(None, ('wide', 'narrow')), may hold values from -4 to 4
- accelerations: float32 [3, 131072], P(None, ('wide', 'narrow')), may hold values from -3 to 3
- jerk_terms: float32 [3, 131072], P(None, ('wide', 'narrow')), may hold values from -6 to 6
- masses: float32 [131072], P(('wide', 'narrow')), may hold values from 7.6293946e-07 to 7.6293945e-05
- levels: int32 [131072], P(('wide', 'narrow')), may hold values from 0 to 3
- active: int32 [4, 4096], P(None, ('wide', 'narrow')), may hold values from 0 to 256, as said below
Outputs:
- new_positions: float32 [3, 131072], P(None, ('wide', 'narrow'))
- new_velocities: float32 [3, 131072], P(None, ('wide', 'narrow'))
- new_accelerations: float32 [3, 131072], P(None, ('wide', 'narrow'))
- new_jerks: float32 [3, 131072], P(None, ('wide', 'narrow'))
- slot_terms: float32 [4, 12, 4096], P(None, None, ('wide', 'narrow'))
The draws below stay inside these ranges and needn't reach their ends.
Inputs may be any that keep to these rules, and one draw needn't show every extreme that they name: `active`: in each step and block the named stars are distinct and fill the block's first slots; every block names at least one star, and in every step some block fills all 8 slots.
All inputs are finite; a program needn't handle non-finite values.
Results may differ from the reference program's by a relative error of at most 0.0007.
Values sent between devices are 32-bit elements; how exact they have to be, the bound alone decides.
No kernel may reach another device: no remote copies, remote signals or barrier semaphores. Data moves between devices by JAX's collectives and lax.ppermute only.
A program may use at most 64 MiB of HBM per device.

```python
import math
import jax
import jax.numpy as jnp
from jax import lax

S_DEV = 256
CAP = 8
STEPS = 4
NSTARS = 131072
SLOTS = 4096
DEVICES = 512


def draw_active(key, part):
    key = jax.random.fold_in(key, 11)
    key_count, key_full, key_order = jax.random.split(key, 3)
    counts = jax.random.randint(key_count, (STEPS, DEVICES), 1, CAP + 1)
    fullest = jax.random.randint(key_full, (STEPS, 1), 0, DEVICES)
    counts = jnp.where(jnp.arange(DEVICES)[None, :] == fullest, CAP, counts)
    scores = jax.random.randint(key_order, (STEPS, DEVICES, S_DEV), 0, (1 << 30) // S_DEV) * S_DEV + jnp.arange(S_DEV)[None, None, :]
    order = jnp.argsort(scores, axis=-1)[:, :, :CAP].astype(jnp.int32)
    picked = jnp.where(jnp.arange(CAP)[None, None, :] < counts[:, :, None], order, S_DEV)
    return picked.reshape(STEPS, DEVICES * CAP).astype(jnp.int32)


def with_ends(drawn, rng, low, high):
    index_at = [jax.random.randint(jax.random.fold_in(rng, axis), (), 0, length) for axis, length in enumerate(drawn.shape)]
    longest = drawn.shape.index(max(drawn.shape))
    beside = index_at[:longest] + [(index_at[longest] + 1) % drawn.shape[longest]] + index_at[longest + 1:]
    return drawn.at[tuple(index_at)].set(low).at[tuple(beside)].set(high)


def block_levels(stream_key, dims, cuts, smallest, high):
    gain, own = 1.0, jax.random.fold_in(stream_key, 6)
    for axis_at, shards_of in cuts:
        steps = jnp.exp(jax.random.uniform(jax.random.fold_in(own, axis_at), (shards_of,), jnp.float32, smallest / len(cuts), high / len(cuts)))
        gain = gain * jnp.repeat(steps, dims[axis_at] // shards_of).reshape([-1 if axis == axis_at else 1 for axis in range(len(dims))])
    return gain


def centred(rng, shape, spread, bound, cuts=(), dtype=jnp.bfloat16):
    result = spread * jax.random.normal(rng, shape, jnp.float32)
    if cuts:
        result = result * block_levels(rng, shape, cuts, -0.22, 0.18)
    return jnp.clip(result, -bound, bound).astype(dtype)


def setup_inputs(seed: int = 0) -> dict:
    keys = jax.random.split(jax.random.key(seed), 8)
    positions = centred(keys[0], (3, NSTARS), 1.0, 6.0, ((1, 512),), jnp.float32)
    velocities = centred(keys[1], (3, NSTARS), 0.5, 4.0, ((1, 512),), jnp.float32)
    accelerations = centred(keys[2], (3, NSTARS), 0.3, 3.0, ((1, 512),), jnp.float32)
    jerk_terms = centred(keys[3], (3, NSTARS), 1.0, 6.0, ((1, 512),), jnp.float32)
    masses = jnp.clip(jnp.exp(math.log(7.62939453125e-05) - 4.6051702 * jax.random.uniform(keys[4], (NSTARS,), jnp.float32) ** block_levels(keys[4], (NSTARS,), ((0, 512),), -0.2, 0.2)), 7.629394644936838e-07, 7.62939453125e-05)
    levels = with_ends(jax.random.randint(keys[5], (NSTARS,), 0, 4), jax.random.fold_in(keys[5], 1), 0, 3).astype(jnp.int32)
    active = draw_active(jax.random.fold_in(keys[7], 71), 0)
    return dict(positions=positions, velocities=velocities, accelerations=accelerations, jerk_terms=jerk_terms, masses=masses, levels=levels, active=active)


step_size = 1.0 / 32.0
softening = 2.5e-05

def predict(positions, velocities, accelerations, jerk_terms, elapsed):
    ahead_pos = positions + elapsed * (velocities + elapsed * (accelerations * 0.5 + elapsed * jerk_terms / 6.0))
    ahead_vel = velocities + elapsed * (accelerations + elapsed * jerk_terms * 0.5)
    return (ahead_pos, ahead_vel)

def pair_sums(targets, source_pos, source_vel, masses):
    delta_x = source_pos[:, None, :] - targets[0:3, :, None]
    delta_v = source_vel[:, None, :] - targets[3:6, :, None]
    radius_sq = lax.optimization_barrier(jnp.sum(delta_x * delta_x, 0)) + softening
    inverse = lax.rsqrt(radius_sq)
    weight = masses[None, :] * inverse * inverse * inverse
    closing = lax.optimization_barrier(jnp.sum(delta_x * delta_v, 0)) / radius_sq
    accel_sum = lax.optimization_barrier(jnp.sum(weight[None] * delta_x, -1))
    jerk_sum = lax.optimization_barrier(jnp.sum(weight[None] * (delta_v - 3.0 * closing[None] * delta_x), -1))
    return jnp.concatenate([accel_sum, jerk_sum], 0)

def correct(old_acc, old_jerk, new_acc, new_jerk, interval):
    diff = old_acc - new_acc
    interval_sq = interval * interval
    second = (-6.0 * diff - interval * (4.0 * old_jerk + 2.0 * new_jerk)) / interval_sq
    third = (12.0 * diff + 6.0 * interval * (old_jerk + new_jerk)) / (interval_sq * interval)
    pos_step = interval_sq * interval_sq * (second / 24.0 + interval * third / 120.0)
    vel_step = interval_sq * interval * (second / 6.0 + interval * third / 24.0)
    return (pos_step, vel_step)

def reference(positions, velocities, accelerations, jerk_terms, masses, levels, active):
    blocks = NSTARS // S_DEV
    times = step_size * (1.0 - jnp.exp2(levels.astype(jnp.float32)))
    slot_block = (jnp.arange(SLOTS) // CAP).astype(jnp.int32)
    recorded = []
    for step in range(STEPS):
        block_time = (step + 1) * step_size
        ahead_pos, ahead_vel = predict(positions, velocities, accelerations, jerk_terms, block_time - times)
        local_ids = active[step]
        filled = local_ids < S_DEV
        global_ids = jnp.where(filled, slot_block * S_DEV + local_ids, NSTARS).astype(jnp.int32)
        safe_ids = jnp.minimum(global_ids, NSTARS - 1)
        targets = jnp.concatenate([ahead_pos[:, safe_ids], ahead_vel[:, safe_ids]], 0)
        source_pos = ahead_pos.reshape(3, blocks, S_DEV).transpose(1, 0, 2)
        source_vel = ahead_vel.reshape(3, blocks, S_DEV).transpose(1, 0, 2)
        source_mass = masses.reshape(blocks, S_DEV)

        def add_block(carry, pieces):
            return (carry + pair_sums(targets, pieces[0], pieces[1], pieces[2]), None)
        summed, unused = lax.scan(add_block, jnp.zeros((6, SLOTS), jnp.float32), (source_pos, source_vel, source_mass))
        new_acc = summed[0:3]
        new_jerk = summed[3:6]
        interval = block_time - times[safe_ids]
        pos_step, vel_step = correct(accelerations[:, safe_ids], jerk_terms[:, safe_ids], new_acc, new_jerk, interval)
        new_pos = ahead_pos[:, safe_ids] + pos_step
        new_vel = ahead_vel[:, safe_ids] + vel_step
        stacked = jnp.concatenate([new_acc, new_jerk, pos_step, vel_step], 0)
        recorded.append(jnp.where(filled[None, :], stacked, jnp.zeros_like(stacked)))
        positions = positions.at[:, global_ids].set(new_pos, mode='drop')
        velocities = velocities.at[:, global_ids].set(new_vel, mode='drop')
        accelerations = accelerations.at[:, global_ids].set(new_acc, mode='drop')
        jerk_terms = jerk_terms.at[:, global_ids].set(new_jerk, mode='drop')
        times = times.at[global_ids].set(jnp.full((SLOTS,), block_time, jnp.float32), mode='drop')
    return (positions, velocities, accelerations, jerk_terms, jnp.stack(recorded, 0))
```

```python
import functools

import jax
import jax.numpy as jnp
from jax import lax
from jax.experimental import pallas as pl
from jax.experimental.pallas import tpu as pltpu
from jax.sharding import Mesh, PartitionSpec as P

step_size = 1.0 / 32.0
softening = 2.5e-05
STEPS = 4
CAP = 8
LANES = 128
HALF = 128
STARS = 256


def predict(x, v, a, j, tau):
    ahead_x = x + tau * (v + tau * (a * 0.5 + tau * j / 6.0))
    ahead_v = v + tau * (a + tau * j * 0.5)
    return ahead_x, ahead_v


def back(x, lanes):
    return pltpu.roll(x, LANES - lanes, 1) if lanes else x


def lane_of(shape):
    return lax.broadcasted_iota(jnp.int32, shape, 1)


def pack_kernel(pos, vel, acc, jerk, mass, levels, active, col_out, row_out, state, rows):
    state[0:3, :] = pos[...]
    state[3:6, :] = vel[...]
    state[6:9, :] = acc[...]
    state[9:12, :] = jerk[...]
    times = step_size * (1.0 - jnp.left_shift(1, levels[...]).astype(jnp.float32))
    state[12:15, :] = jnp.broadcast_to(times, (3, STARS))
    state[15:16, :] = mass[...]
    whole = state[...]
    lane = lane_of((16, LANES))
    diagonal = lane // CAP == lax.broadcasted_iota(jnp.int32, (16, LANES), 0)
    slot = lane % CAP
    star = lane_of((1, STARS))
    for k in range(STEPS):
        table = jnp.zeros((16, LANES), jnp.float32)
        ids = jnp.zeros((1, LANES), jnp.float32)
        for s in range(CAP):
            named = active[k, s]
            column = jnp.sum(jnp.where(star == named, whole, 0.0), axis=1, keepdims=True)
            table = jnp.where(slot == s, column, table)
            ids = jnp.where(slot[0:1] == s, named.astype(jnp.float32), ids)
        rows[k : k + 1, :] = jnp.sum(jnp.where(diagonal, table, 0.0), axis=0, keepdims=True)
        rows[STEPS + k : STEPS + k + 1, :] = ids
    row_out[...] = jnp.broadcast_to(rows[...][None], row_out.shape)
    peers = col_out.shape[0]
    col_out[:, 0:16, :] = jnp.broadcast_to(whole[None, :, :HALF], (peers, 16, HALF))
    col_out[:, 16:32, :] = jnp.broadcast_to(whole[None, :, HALF:], (peers, 16, HALF))


def force_kernel(step, ncol, nrow, *refs):
    block_time = (step + 1) * step_size
    if step == 0:
        raw, target_rows = refs[0], refs[1]
        refs = refs[2:]
    else:
        before, fresh, targets = refs[0], refs[1], refs[2]
        refs = refs[3:]
    if step < STEPS - 1:
        sums_out, state, source, splat, part = refs
    else:
        sums_out, source, splat, part, state = refs

    if step == 0:
        for q in range(14):
            row = 15 if q == 13 else q
            for h in range(2):
                state[q, h * ncol : (h + 1) * ncol, :] = raw[pl.ds(16 * h + row, ncol, stride=32), :]
    else:
        state[...] = before[...]
        changed = fresh[...]
        lane = lane_of((ncol, LANES)).astype(jnp.float32)
        for s in range(CAP):
            named = jnp.broadcast_to(changed[:, 104 + s : 105 + s], (ncol, LANES))
            hits = [named == lane + float(h * HALF) for h in range(2)]
            for q in range(12):
                value = jnp.broadcast_to(changed[:, CAP * q + s : CAP * q + s + 1], (ncol, LANES))
                for h in range(2):
                    at = pl.ds(h * ncol, ncol)
                    state[q, at, :] = jnp.where(hits[h], value, state[q, at, :])
            for h in range(2):
                at = pl.ds(h * ncol, ncol)
                state[12, at, :] = jnp.where(hits[h], step * step_size, state[12, at, :])
    tau = block_time - state[12]
    for c in range(3):
        x, v = predict(state[c], state[3 + c], state[6 + c], state[9 + c], tau)
        source[c] = x
        source[3 + c] = v
    source[6] = state[13]

    z = target_rows[pl.ds(0, nrow, stride=CAP), :] if step == 0 else targets[...]
    x, v = predict(z, back(z, 24), back(z, 48), back(z, 72), block_time - back(z, 96))
    for q in range(6):
        held = x if q < 3 else v
        for s in range(CAP):
            at = CAP * (q % 3) + s
            splat[pl.ds((q * CAP + s) * nrow, nrow), :] = jnp.broadcast_to(
                held[:, at : at + 1], (nrow, LANES)
            )

    count = CAP * nrow
    chunks = 2 * ncol // 8

    def one_target(i, carry):
        g = [jnp.broadcast_to(splat[pl.ds(q * count + i, 1), :], (8, LANES)) for q in range(6)]
        sums = [jnp.zeros((8, LANES), jnp.float32) for _ in range(6)]
        for c in range(chunks):
            at = pl.ds(8 * c, 8)
            dx, dy, dz = (source[q, at, :] - g[q] for q in range(3))
            du, dv, dw = (source[q, at, :] - g[q] for q in range(3, 6))
            radius_sq = (dx * dx + dy * dy + dz * dz) + softening
            inverse = lax.rsqrt(radius_sq)
            inverse_sq = inverse * inverse
            weight = source[6, at, :] * inverse * inverse_sq
            closing = (dx * du + dy * dv + dz * dw) * (3.0 * inverse_sq)
            sums[0] = sums[0] + weight * dx
            sums[1] = sums[1] + weight * dy
            sums[2] = sums[2] + weight * dz
            sums[3] = sums[3] + weight * (du - closing * dx)
            sums[4] = sums[4] + weight * (dv - closing * dy)
            sums[5] = sums[5] + weight * (dw - closing * dz)
        for q in range(6):
            part[pl.ds(q * count + i, 1), :] = jnp.sum(sums[q], axis=0, keepdims=True)
        return carry

    lax.fori_loop(0, count, one_target, 0, unroll=2)

    lane = lane_of((nrow, LANES))
    total = jnp.zeros((nrow, LANES), jnp.float32)
    for q in range(6):
        for s in range(CAP):
            line = part[pl.ds((q * CAP + s) * nrow, nrow), :]
            total = jnp.where(lane == CAP * q + s, jnp.sum(line, axis=1, keepdims=True), total)
    sums_out[...] = jnp.broadcast_to(total[None], sums_out.shape)


def correct(old_acc, old_jerk, new_acc, new_jerk, interval):
    diff = old_acc - new_acc
    interval_sq = interval * interval
    second = (-6.0 * diff - interval * (4.0 * old_jerk + 2.0 * new_jerk)) / interval_sq
    third = (12.0 * diff + 6.0 * interval * (old_jerk + new_jerk)) / (interval_sq * interval)
    pos_step = interval_sq * interval_sq * (second / 24.0 + interval * third / 120.0)
    vel_step = interval_sq * interval * (second / 6.0 + interval * third / 24.0)
    return (pos_step, vel_step)


def turn(x, d, slot):
    if d == 0:
        return x
    return jnp.where(slot < CAP - d, pltpu.roll(x, LANES - d, 1), pltpu.roll(x, CAP - d, 1))


def spread(line, diagonal):
    x = jnp.where(diagonal, jnp.broadcast_to(line, (16, LANES)), 0.0)
    for shift in (64, 32, 16, 8):
        x = x + pltpu.roll(x, shift, 1)
    return x


def correct_kernel(step, nrow, me_of, *refs):
    block_time = (step + 1) * step_size
    gathered, target_rows = refs[0], refs[1]
    refs = refs[2:]
    if step > 0:
        targets, refs = refs[0], refs[1:]
        earlier, refs = refs[:step], refs[step:]
    else:
        earlier = ()
    last = step == STEPS - 1
    if last:
        term_rows, refs = refs[: STEPS - 1], refs[STEPS - 1 :]
        pos, vel, acc, jerk, active = refs[:5]
        new_pos, new_vel, new_acc, new_jerk, terms_out, state, keep = refs[5:]
    else:
        corrected_out, next_out, fresh_out, terms_out, keep = refs
    me = me_of()

    total = gathered[0]
    for p in range(1, nrow):
        total = total + gathered[p]
    z = target_rows[pl.ds(0, nrow, stride=CAP), :] if step == 0 else targets[...]
    ids = target_rows[pl.ds(STEPS + step, nrow, stride=CAP), :]
    lane = lane_of((nrow, LANES))
    slot = lane % CAP
    tau = block_time - back(z, 96)
    old_acc, old_jerk = back(z, 48), back(z, 72)
    x, v = predict(z, back(z, 24), old_acc, old_jerk, tau)
    new_a, new_j = total, back(total, 24)
    pos_step, vel_step = correct(old_acc, old_jerk, new_a, new_j, tau)

    def lay(*parts):
        out = parts[-1]
        for n in reversed(range(len(parts) - 1)):
            piece = pltpu.roll(parts[n], 24 * n, 1) if n else parts[n]
            out = jnp.where(lane < 24 * (n + 1), piece, out)
        return out

    rest = jnp.where(lane < 120, block_time, z)
    corrected = lay(x + pos_step, v + vel_step, new_a, new_j, rest)
    terms = lay(new_a, new_j, pos_step, vel_step, jnp.zeros_like(z))
    terms = jnp.where(ids < float(STARS), terms, 0.0)

    keep[0] = terms
    own_terms = keep[0, pl.ds(me, 1), :]
    if not last:
        terms_out[...] = own_terms
        corrected_out[...] = corrected
        keep[1] = jnp.where((lane >= 104) & (lane < 112), ids, corrected)
        fresh_out[...] = jnp.broadcast_to(keep[1, pl.ds(me, 1), :][None], fresh_out.shape)
        following = target_rows[pl.ds(step + 1, nrow, stride=CAP), :]
        wanted = target_rows[pl.ds(STEPS + step + 1, nrow, stride=CAP), :]
        real = wanted < float(STARS)
        for j in range(step + 1):
            values = earlier[j][...] if j < step else corrected
            names = target_rows[pl.ds(STEPS + j, nrow, stride=CAP), :]
            for d in range(CAP):
                hit = (turn(names, d, slot) == wanted) & real
                following = jnp.where(hit, turn(values, d, slot), following)
        next_out[...] = following
        return

    keep[1] = corrected
    wide_lane = lane_of((16, LANES))
    diagonal = wide_lane // CAP == lax.broadcasted_iota(jnp.int32, (16, LANES), 0)
    state[0:3, :] = pos[...]
    state[3:6, :] = vel[...]
    state[6:9, :] = acc[...]
    state[9:12, :] = jerk[...]
    state[12:16, :] = jnp.zeros((4, STARS), jnp.float32)
    whole = state[...]
    star = lane_of((16, STARS))
    for j in range(STEPS):
        line = earlier[j][pl.ds(me, 1), :] if j < step else keep[1, pl.ds(me, 1), :]
        columns = spread(line, diagonal)
        for s in range(CAP):
            whole = jnp.where(star == active[j, s], columns[:, s : s + 1], whole)
        line = term_rows[j][...] if j < step else own_terms
        terms_out[j] = spread(line, diagonal)[0:12, 0:CAP]
    new_pos[...] = whole[0:3, :]
    new_vel[...] = whole[3:6, :]
    new_acc[...] = whole[6:9, :]
    new_jerk[...] = whole[9:12, :]


def struct(*shape):
    return jax.ShapeDtypeStruct(shape, jnp.float32)


def scratch(*shape):
    return pltpu.VMEM(shape, jnp.float32)


vmem = pl.BlockSpec(memory_space=pltpu.VMEM)
smem = pl.BlockSpec(memory_space=pltpu.SMEM)


def send_all(x, axes):
    return lax.all_to_all(x, axes, split_axis=0, concat_axis=0, tiled=True)


def body(ncol, nrow, narrow, pos, vel, acc, jerk, masses, levels, active):
    def me_of():
        return lax.axis_index("core") * narrow + lax.axis_index("narrow")

    col_block, row_block = pl.pallas_call(
        pack_kernel,
        out_shape=(struct(ncol, 32, LANES), struct(nrow, 8, LANES)),
        in_specs=[vmem] * 6 + [smem],
        out_specs=(vmem, vmem),
        scratch_shapes=[scratch(16, STARS), scratch(8, LANES)],
    )(pos, vel, acc, jerk, masses.reshape(1, STARS), levels.reshape(1, STARS), active)
    target_rows = send_all(row_block, ("core", "narrow")).reshape(nrow * 8, LANES)
    raw = send_all(col_block, "across").reshape(ncol * 32, LANES)

    state = fresh = targets = None
    corrected, terms = [], []
    for step in range(STEPS):
        last = step == STEPS - 1
        operands = (raw, target_rows) if step == 0 else (state, fresh, targets)
        state_shape = (14, 2 * ncol, LANES)
        work = [scratch(7, 2 * ncol, LANES), scratch(48 * nrow, LANES), scratch(48 * nrow, LANES)]
        outs = (struct(nrow, nrow, LANES),)
        if last:
            work.append(scratch(*state_shape))
        else:
            outs += (struct(*state_shape),)
        result = pl.pallas_call(
            functools.partial(force_kernel, step, ncol, nrow),
            out_shape=outs,
            in_specs=[vmem] * len(operands),
            out_specs=(vmem,) * len(outs),
            scratch_shapes=work,
        )(*operands)
        partial_sums = result[0]
        state = None if last else result[1]
        gathered = send_all(partial_sums, ("core", "narrow"))
        operands = [gathered, target_rows]
        if step > 0:
            operands += [targets, *corrected]
        in_specs = [vmem] * len(operands)
        work = [scratch(2, nrow, LANES)]
        if last:
            operands += [*terms, pos, vel, acc, jerk, active]
            in_specs += [vmem] * (STEPS + 3) + [smem]
            outs = (struct(3, STARS),) * 4 + (struct(STEPS, 12, CAP),)
            work = [scratch(16, STARS)] + work
        else:
            outs = (
                struct(nrow, LANES),
                struct(nrow, LANES),
                struct(ncol, 1, LANES),
                struct(1, LANES),
            )
        result = pl.pallas_call(
            functools.partial(correct_kernel, step, nrow, me_of),
            out_shape=outs,
            in_specs=in_specs,
            out_specs=(vmem,) * len(outs),
            scratch_shapes=work,
        )(*operands)
        if last:
            return result
        new_rows, targets, fresh, own_terms = result
        corrected.append(new_rows)
        terms.append(own_terms)
        fresh = send_all(fresh, "across").reshape(ncol, LANES)


def solution(mesh):
    wide, narrow = mesh.shape["wide"], mesh.shape["narrow"]
    ncol, nrow = wide // 2, 2 * narrow
    finer = Mesh(mesh.devices.reshape(ncol, 2, narrow), ("across", "core", "narrow"))
    every = ("across", "core", "narrow")
    in_specs = (P(None, every),) * 4 + (P(every), P(every), P(None, every))
    out_specs = (P(None, every),) * 4 + (P(None, None, every),)
    return jax.shard_map(
        functools.partial(body, ncol, nrow, narrow),
        mesh=finer,
        in_specs=in_specs,
        out_specs=out_specs,
        check_vma=False,
    )
```

```python
import functools

import jax
import jax.numpy as jnp
from jax import lax
from jax.experimental import pallas as pl
from jax.experimental.pallas import tpu as pltpu
from jax.sharding import Mesh, PartitionSpec as P

step_size = 1.0 / 32.0
softening = 2.5e-05
STEPS = 4
CAP = 8
LANES = 128
HALF = 128
STARS = 256


def predict(x, v, a, j, tau):
    ahead_x = x + tau * (v + tau * (a * 0.5 + tau * j / 6.0))
    ahead_v = v + tau * (a + tau * j * 0.5)
    return ahead_x, ahead_v


def back(x, lanes):
    return pltpu.roll(x, LANES - lanes, 1) if lanes else x


def lane_of(shape):
    return lax.broadcasted_iota(jnp.int32, shape, 1)


def fetch(sources, held, sems):
    copies = [pltpu.make_async_copy(a, b, sems.at[n]) for n, (a, b) in enumerate(zip(sources, held))]
    for copy in copies:
        copy.start()
    return copies


def pack_kernel(*refs):
    active, col_out, row_out, *held = refs[6:15]
    state, rows, sems = refs[15:]
    for copy in fetch(refs[:6], held, sems):
        copy.wait()
    pos, vel, acc, jerk, mass, levels = held
    state[0:3, :] = pos[...]
    state[3:6, :] = vel[...]
    state[6:9, :] = acc[...]
    state[9:12, :] = jerk[...]
    times = step_size * (1.0 - jnp.left_shift(1, levels[...]).astype(jnp.float32))
    state[12:15, :] = jnp.broadcast_to(times, (3, STARS))
    state[15:16, :] = mass[...]
    whole = state[...]
    lane = lane_of((16, LANES))
    diagonal = lane // CAP == lax.broadcasted_iota(jnp.int32, (16, LANES), 0)
    slot = lane % CAP
    star = lane_of((1, STARS))
    for k in range(STEPS):
        table = jnp.zeros((16, LANES), jnp.float32)
        ids = jnp.zeros((1, LANES), jnp.float32)
        for s in range(CAP):
            named = active[k, s]
            column = jnp.sum(jnp.where(star == named, whole, 0.0), axis=1, keepdims=True)
            table = jnp.where(slot == s, column, table)
            ids = jnp.where(slot[0:1] == s, named.astype(jnp.float32), ids)
        rows[k : k + 1, :] = jnp.sum(jnp.where(diagonal, table, 0.0), axis=0, keepdims=True)
        rows[STEPS + k : STEPS + k + 1, :] = ids
    row_out[...] = jnp.broadcast_to(rows[...][None], row_out.shape)
    peers = col_out.shape[0]
    col_out[:, 0:16, :] = jnp.broadcast_to(whole[None, :, :HALF], (peers, 16, HALF))
    col_out[:, 16:32, :] = jnp.broadcast_to(whole[None, :, HALF:], (peers, 16, HALF))


def force_kernel(step, ncol, nrow, *refs):
    block_time = (step + 1) * step_size
    if step == 0:
        raw, target_rows = refs[0], refs[1]
        refs = refs[2:]
    else:
        before, fresh, targets = refs[0], refs[1], refs[2]
        refs = refs[3:]
    if step < STEPS - 1:
        sums_out, state, source, splat, part = refs
    else:
        sums_out, source, splat, part, state = refs

    if step == 0:
        for q in range(14):
            row = 15 if q == 13 else q
            for h in range(2):
                state[q, h * ncol : (h + 1) * ncol, :] = raw[pl.ds(16 * h + row, ncol, stride=32), :]
    else:
        state[...] = before[...]
        changed = fresh[...]
        lane = lane_of((ncol, LANES)).astype(jnp.float32)
        for s in range(CAP):
            named = jnp.broadcast_to(changed[:, 104 + s : 105 + s], (ncol, LANES))
            hits = [named == lane + float(h * HALF) for h in range(2)]
            for q in range(12):
                value = jnp.broadcast_to(changed[:, CAP * q + s : CAP * q + s + 1], (ncol, LANES))
                for h in range(2):
                    at = pl.ds(h * ncol, ncol)
                    state[q, at, :] = jnp.where(hits[h], value, state[q, at, :])
            for h in range(2):
                at = pl.ds(h * ncol, ncol)
                state[12, at, :] = jnp.where(hits[h], step * step_size, state[12, at, :])
    tau = block_time - state[12]
    for c in range(3):
        x, v = predict(state[c], state[3 + c], state[6 + c], state[9 + c], tau)
        source[c] = x
        source[3 + c] = v
    source[6] = state[13]

    z = target_rows[pl.ds(0, nrow, stride=CAP), :] if step == 0 else targets[...]
    x, v = predict(z, back(z, 24), back(z, 48), back(z, 72), block_time - back(z, 96))
    for q in range(6):
        held = x if q < 3 else v
        for s in range(CAP):
            at = CAP * (q % 3) + s
            splat[pl.ds((q * CAP + s) * nrow, nrow), :] = jnp.broadcast_to(
                held[:, at : at + 1], (nrow, LANES)
            )

    count = CAP * nrow
    chunks = 2 * ncol // 8

    def one_target(i, carry):
        g = [jnp.broadcast_to(splat[pl.ds(q * count + i, 1), :], (8, LANES)) for q in range(6)]
        sums = [jnp.zeros((8, LANES), jnp.float32) for _ in range(6)]
        for c in range(chunks):
            at = pl.ds(8 * c, 8)
            dx, dy, dz = (source[q, at, :] - g[q] for q in range(3))
            du, dv, dw = (source[q, at, :] - g[q] for q in range(3, 6))
            radius_sq = (dx * dx + dy * dy + dz * dz) + softening
            inverse = lax.rsqrt(radius_sq)
            inverse_sq = inverse * inverse
            weight = source[6, at, :] * inverse * inverse_sq
            closing = (dx * du + dy * dv + dz * dw) * (3.0 * inverse_sq)
            sums[0] = sums[0] + weight * dx
            sums[1] = sums[1] + weight * dy
            sums[2] = sums[2] + weight * dz
            sums[3] = sums[3] + weight * (du - closing * dx)
            sums[4] = sums[4] + weight * (dv - closing * dy)
            sums[5] = sums[5] + weight * (dw - closing * dz)
        for q in range(6):
            part[pl.ds(q * count + i, 1), :] = jnp.sum(sums[q], axis=0, keepdims=True)
        return carry

    lax.fori_loop(0, count, one_target, 0, unroll=8)

    half = nrow // 2
    lane = lane_of((half, LANES))
    total = jnp.zeros((half, LANES), jnp.float32)
    for q in range(6):
        for s in range(CAP):
            for h in range(2):
                line = part[pl.ds((q * CAP + s) * nrow + h * half, half), :]
                line = jnp.sum(line, axis=1, keepdims=True)
                total = jnp.where(lane == 64 * h + CAP * q + s, line, total)
    sums_out[...] = jnp.broadcast_to(total[None], sums_out.shape)


def correct(old_acc, old_jerk, new_acc, new_jerk, interval):
    diff = old_acc - new_acc
    interval_sq = interval * interval
    second = (-6.0 * diff - interval * (4.0 * old_jerk + 2.0 * new_jerk)) / interval_sq
    third = (12.0 * diff + 6.0 * interval * (old_jerk + new_jerk)) / (interval_sq * interval)
    pos_step = interval_sq * interval_sq * (second / 24.0 + interval * third / 120.0)
    vel_step = interval_sq * interval * (second / 6.0 + interval * third / 24.0)
    return (pos_step, vel_step)


def turn(x, d, slot):
    if d == 0:
        return x
    return jnp.where(slot < CAP - d, pltpu.roll(x, LANES - d, 1), pltpu.roll(x, CAP - d, 1))


def spread(line, diagonal):
    x = jnp.where(diagonal, jnp.broadcast_to(line, (16, LANES)), 0.0)
    for shift in (64, 32, 16, 8):
        x = x + pltpu.roll(x, shift, 1)
    return x


def correct_kernel(step, nrow, me_of, *refs):
    block_time = (step + 1) * step_size
    gathered, target_rows = refs[0], refs[1]
    refs = refs[2:]
    if step > 0:
        targets, refs = refs[0], refs[1:]
        earlier, refs = refs[:step], refs[step:]
    else:
        earlier = ()
    last = step == STEPS - 1
    if last:
        term_rows, refs = refs[: STEPS - 1], refs[STEPS - 1 :]
        started, active = refs[:4], refs[4]
        new_pos, new_vel, new_acc, new_jerk, terms_out, state, *held, sems, keep = refs[5:]
        copies = fetch(started, held, sems)
    else:
        corrected_out, next_out, fresh_out, terms_out, keep = refs
    me = me_of()

    total = gathered[0]
    for p in range(1, nrow):
        total = total + gathered[p]
    total = jnp.concatenate([total, back(total, 64)], axis=0)
    z = target_rows[pl.ds(0, nrow, stride=CAP), :] if step == 0 else targets[...]
    ids = target_rows[pl.ds(STEPS + step, nrow, stride=CAP), :]
    lane = lane_of((nrow, LANES))
    slot = lane % CAP
    tau = block_time - back(z, 96)
    old_acc, old_jerk = back(z, 48), back(z, 72)
    x, v = predict(z, back(z, 24), old_acc, old_jerk, tau)
    new_a, new_j = total, back(total, 24)
    pos_step, vel_step = correct(old_acc, old_jerk, new_a, new_j, tau)

    def lay(*parts):
        out = parts[-1]
        for n in reversed(range(len(parts) - 1)):
            piece = pltpu.roll(parts[n], 24 * n, 1) if n else parts[n]
            out = jnp.where(lane < 24 * (n + 1), piece, out)
        return out

    rest = jnp.where(lane < 120, block_time, z)
    corrected = lay(x + pos_step, v + vel_step, new_a, new_j, rest)
    terms = lay(new_a, new_j, pos_step, vel_step, jnp.zeros_like(z))
    terms = jnp.where(ids < float(STARS), terms, 0.0)

    keep[0] = terms
    own_terms = keep[0, pl.ds(me, 1), :]
    if not last:
        terms_out[...] = own_terms
        corrected_out[...] = corrected
        keep[1] = jnp.where((lane >= 104) & (lane < 112), ids, corrected)
        fresh_out[...] = jnp.broadcast_to(keep[1, pl.ds(me, 1), :][None], fresh_out.shape)
        following = target_rows[pl.ds(step + 1, nrow, stride=CAP), :]
        wanted = target_rows[pl.ds(STEPS + step + 1, nrow, stride=CAP), :]
        real = wanted < float(STARS)
        for j in range(step + 1):
            values = earlier[j][...] if j < step else corrected
            names = target_rows[pl.ds(STEPS + j, nrow, stride=CAP), :]
            for d in range(CAP):
                hit = (turn(names, d, slot) == wanted) & real
                following = jnp.where(hit, turn(values, d, slot), following)
        next_out[...] = following
        return

    keep[1] = corrected
    wide_lane = lane_of((16, LANES))
    diagonal = wide_lane // CAP == lax.broadcasted_iota(jnp.int32, (16, LANES), 0)
    for copy in copies:
        copy.wait()
    for n in range(4):
        state[3 * n : 3 * n + 3, :] = held[n][...]
    state[12:16, :] = jnp.zeros((4, STARS), jnp.float32)
    whole = state[...]
    star = lane_of((16, STARS))
    for j in range(STEPS):
        line = earlier[j][pl.ds(me, 1), :] if j < step else keep[1, pl.ds(me, 1), :]
        columns = spread(line, diagonal)
        for s in range(CAP):
            whole = jnp.where(star == active[j, s], columns[:, s : s + 1], whole)
        line = term_rows[j][...] if j < step else own_terms
        terms_out[j] = jnp.transpose(spread(line, diagonal))[0:CAP, 0:12]
    new_pos[...] = whole[0:3, :]
    new_vel[...] = whole[3:6, :]
    new_acc[...] = whole[6:9, :]
    new_jerk[...] = whole[9:12, :]


def struct(*shape):
    return jax.ShapeDtypeStruct(shape, jnp.float32)


def scratch(*shape):
    return pltpu.VMEM(shape, jnp.float32)


vmem = pl.BlockSpec(memory_space=pltpu.VMEM)
hbm = pl.BlockSpec(memory_space=pltpu.HBM)
smem = pl.BlockSpec(memory_space=pltpu.SMEM)


params = pltpu.CompilerParams(vmem_limit_bytes=8 << 20)


def send_all(x, axes):
    return lax.all_to_all(x, axes, split_axis=0, concat_axis=0, tiled=True)


def body(ncol, nrow, narrow, pos, vel, acc, jerk, masses, levels, active):
    masses, levels = masses.reshape(1, STARS), levels.reshape(1, STARS)
    pos, vel, acc, jerk, masses, levels, active = (
        pltpu.with_memory_space_constraint(a, pltpu.HBM)
        for a in (pos, vel, acc, jerk, masses, levels, active)
    )

    def me_of():
        return lax.axis_index("core") * narrow + lax.axis_index("narrow")

    col_block, row_block = pl.pallas_call(
        pack_kernel,
        out_shape=(struct(ncol, 32, LANES), struct(nrow, 8, LANES)),
        in_specs=[hbm] * 6 + [smem],
        out_specs=(vmem, vmem),
        scratch_shapes=[scratch(3, STARS)] * 4
        + [scratch(1, STARS), pltpu.VMEM((1, STARS), jnp.int32)]
        + [scratch(16, STARS), scratch(8, LANES), pltpu.SemaphoreType.DMA((6,))],
        compiler_params=params,
    )(pos, vel, acc, jerk, masses, levels, active)
    target_rows = send_all(row_block, ("core", "narrow")).reshape(nrow * 8, LANES)
    raw = send_all(col_block, "across").reshape(ncol * 32, LANES)

    state = fresh = targets = None
    corrected, terms = [], []
    for step in range(STEPS):
        last = step == STEPS - 1
        operands = (raw, target_rows) if step == 0 else (state, fresh, targets)
        state_shape = (14, 2 * ncol, LANES)
        work = [scratch(7, 2 * ncol, LANES), scratch(48 * nrow, LANES), scratch(48 * nrow, LANES)]
        outs = (struct(nrow, nrow // 2, LANES),)
        if last:
            work.append(scratch(*state_shape))
        else:
            outs += (struct(*state_shape),)
        result = pl.pallas_call(
            functools.partial(force_kernel, step, ncol, nrow),
            out_shape=outs,
            in_specs=[vmem] * len(operands),
            out_specs=(vmem,) * len(outs),
            scratch_shapes=work,
            compiler_params=params,
        )(*operands)
        partial_sums = result[0]
        state = None if last else result[1]
        gathered = send_all(partial_sums, ("core", "narrow"))
        operands = [gathered, target_rows]
        if step > 0:
            operands += [targets, *corrected]
        in_specs = [vmem] * len(operands)
        work = [scratch(2, nrow, LANES)]
        if last:
            operands += [*terms, pos, vel, acc, jerk, active]
            in_specs += [vmem] * (STEPS - 1) + [hbm] * 4 + [smem]
            outs = (struct(3, STARS),) * 4 + (struct(STEPS, CAP, 12),)
            work = [scratch(16, STARS)] + [scratch(3, STARS)] * 4 + [pltpu.SemaphoreType.DMA((4,))] + work
        else:
            outs = (
                struct(nrow, LANES),
                struct(nrow, LANES),
                struct(ncol, 1, LANES),
                struct(1, LANES),
            )
        result = pl.pallas_call(
            functools.partial(correct_kernel, step, nrow, me_of),
            out_shape=outs,
            in_specs=in_specs,
            out_specs=(vmem,) * len(outs),
            scratch_shapes=work,
            compiler_params=params,
        )(*operands)
        if last:
            return (*result[:4], jnp.swapaxes(result[4], 1, 2))
        new_rows, targets, fresh, own_terms = result
        corrected.append(new_rows)
        terms.append(own_terms)
        fresh = send_all(fresh, "across").reshape(ncol, LANES)


def solution(mesh):
    wide, narrow = mesh.shape["wide"], mesh.shape["narrow"]
    ncol, nrow = wide // 2, 2 * narrow
    finer = Mesh(mesh.devices.reshape(ncol, 2, narrow), ("across", "core", "narrow"))
    every = ("across", "core", "narrow")
    in_specs = (P(None, every),) * 4 + (P(every), P(every), P(None, every))
    out_specs = (P(None, every),) * 4 + (P(None, None, every),)
    return jax.shard_map(
        functools.partial(body, ncol, nrow, narrow),
        mesh=finer,
        in_specs=in_specs,
        out_specs=out_specs,
        check_vma=False,
    )
```

```python
import functools

import jax
import jax.numpy as jnp
from jax import lax
from jax.experimental import pallas as pl
from jax.experimental.pallas import tpu as pltpu
from jax.sharding import Mesh, PartitionSpec as P

step_size = 1.0 / 32.0
softening = 2.5e-05
STEPS = 4
CAP = 8
LANES = 128
STARS = 256

NROW = 16
TARGETS = NROW * CAP
GROUPS = TARGETS // 8
AT_ONCE = 8
LIST = TARGETS + 32


def predict(x, v, a, j, tau):
    ahead_x = x + tau * (v + tau * (a * 0.5 + tau * j / 6.0))
    ahead_v = v + tau * (a + tau * j * 0.5)
    return ahead_x, ahead_v


def back(x, lanes):
    return pltpu.roll(x, LANES - lanes, 1) if lanes else x


def lane_of(shape):
    return lax.broadcasted_iota(jnp.int32, shape, 1)


def row_of(shape):
    return lax.broadcasted_iota(jnp.int32, shape, 0)


def turn(x, d):
    if d == 0:
        return x
    slot = lane_of(x.shape) % CAP
    return jnp.where(slot < CAP - d, pltpu.roll(x, LANES - d, 1), pltpu.roll(x, CAP - d, 1))


def fetch(sources, held, sems):
    copies = [pltpu.make_async_copy(a, b, sems.at[n]) for n, (a, b) in enumerate(zip(sources, held))]
    for copy in copies:
        copy.start()
    return copies


def pack_kernel(*refs):
    active, block_out, row_out, state, *held = refs[6:16]
    block, rows, sems = refs[16:]
    for copy in fetch(refs[:6], held, sems):
        copy.wait()
    pos, vel, acc, jerk, mass, levels = held
    for n, part in enumerate((pos, vel, acc, jerk)):
        state[3 * n : 3 * n + 3, :] = part[...]
    times = step_size * (1.0 - jnp.left_shift(1, levels[...]).astype(jnp.float32))
    state[12:15, :] = jnp.broadcast_to(times, (3, STARS))
    state[15:16, :] = mass[...]
    whole = state[...]
    lane = lane_of((1, LANES))
    names = jnp.full((1, LANES), STARS, jnp.int32)
    for k in range(STEPS):
        for s in range(CAP):
            names = jnp.where(lane == CAP * k + s, active[k, s], names)
    block[0:16, :] = whole[:, :LANES]
    block[16:32, :] = whole[:, LANES:]
    block[13:14, :] = names.astype(jnp.float32)
    block_out[...] = jnp.broadcast_to(block[...][None], block_out.shape)
    lane = lane_of((16, LANES))
    diagonal = lane // CAP == row_of((16, LANES))
    slot = lane % CAP
    star = lane_of((1, STARS))
    for k in range(STEPS):
        table = jnp.zeros((16, LANES), jnp.float32)
        names = jnp.zeros((1, LANES), jnp.float32)
        for s in range(CAP):
            named = active[k, s]
            column = jnp.sum(jnp.where(star == named, whole, 0.0), axis=1, keepdims=True)
            table = jnp.where(slot == s, column, table)
            names = jnp.where(slot[0:1] == s, named.astype(jnp.float32), names)
        rows[k : k + 1, :] = jnp.sum(jnp.where(diagonal, table, 0.0), axis=0, keepdims=True)
        rows[STEPS + k : STEPS + k + 1, :] = names
    row_out[...] = jnp.broadcast_to(rows[...][None], row_out.shape)


def plan_kernel(scalars, target_rows, lists, splat):
    for k in range(STEPS):

        def peer(r, n):
            for s in range(CAP):
                lists[k, n] = NROW * s + r
                n = n + jnp.where(scalars[CAP * r + STEPS + k, s] < float(STARS), 1, 0)
            return n

        n = lax.fori_loop(0, NROW, peer, 0)
        for u in range(AT_ONCE):
            lists[k, n + u] = 0
        lists[k, LIST - 1] = n
    spread_targets(target_rows_at(target_rows, 0), splat, step_size)


def predict_sources(raw, source, block_time, ncol):
    for h in range(2):
        at = pl.ds(h * ncol, ncol)

        def load(q):
            return raw[pl.ds(16 * h + q, ncol, stride=32), :]

        tau = block_time - load(12)
        for c in range(3):
            x, v = predict(load(c), load(3 + c), load(6 + c), load(9 + c), tau)
            source[c, at, :] = x
            source[3 + c, at, :] = v


def spread_targets(z, splat, block_time):
    x, v = predict(z, back(z, 24), back(z, 48), back(z, 72), block_time - back(z, 96))
    for q in range(6):
        held = x if q < 3 else v
        for s in range(CAP):
            at = CAP * (q % 3) + s
            splat[pl.ds((q * CAP + s) * NROW, NROW), :] = jnp.broadcast_to(
                held[:, at : at + 1], (NROW, LANES)
            )


def add_pairs(sums, sources, target):
    dx, dy, dz, du, dv, dw = (sources[q] - target[q] for q in range(6))
    radius_sq = (dx * dx + dy * dy + dz * dz) + softening
    inverse = lax.rsqrt(radius_sq)
    inverse_sq = inverse * inverse
    weight = sources[6] * inverse * inverse_sq
    closing = (dx * du + dy * dv + dz * dw) * (3.0 * inverse_sq)
    return (
        sums[0] + weight * dx,
        sums[1] + weight * dy,
        sums[2] + weight * dz,
        sums[3] + weight * (du - closing * dx),
        sums[4] + weight * (dv - closing * dy),
        sums[5] + weight * (dw - closing * dz),
    )


def wide_row(ref, q, r):
    return jnp.broadcast_to(ref[q, pl.ds(r, 1), :], (8, LANES))


def sum_listed(source, splat, part, lists, step):
    chunks = source.shape[1] // 8
    part[...] = jnp.zeros(part.shape, jnp.float32)
    zero = jnp.zeros((8, LANES), jnp.float32)

    def some_targets(n, carry):
        for u in range(AT_ONCE):
            i = lists[step, AT_ONCE * n + u]
            target = [
                jnp.broadcast_to(splat[pl.ds(q * TARGETS + i, 1), :], (8, LANES)) for q in range(6)
            ]
            sums = (zero,) * 6
            for c in range(chunks):
                sums = add_pairs(sums, [source[q, pl.ds(8 * c, 8), :] for q in range(7)], target)
            for q in range(6):
                part[pl.ds(q * TARGETS + i, 1), :] = jnp.sum(sums[q], axis=0, keepdims=True)
        return carry

    lax.fori_loop(0, (lists[step, LIST - 1] + AT_ONCE - 1) // AT_ONCE, some_targets, 0)


def pack_sums(part):
    lane = lane_of((8, LANES))
    total = jnp.zeros((8, LANES), jnp.float32)
    for q in range(6):
        for g in range(GROUPS):
            line = jnp.sum(part[pl.ds(q * TARGETS + 8 * g, 8), :], axis=1, keepdims=True)
            total = jnp.where(lane == 64 * (g % 2) + CAP * q + g // 2, line, total)
    return total


def load_masses(raw, ncol):
    return [raw[pl.ds(16 * h + 15, ncol, stride=32), :] for h in range(2)]


def first_force_kernel(ncol, raw, lists_in, splat, sums_out, lists, sem, source, part):
    copy = pltpu.make_async_copy(lists_in, lists, sem)
    copy.start()
    predict_sources(raw, source, step_size, ncol)
    for h, mass in enumerate(load_masses(raw, ncol)):
        source[6, pl.ds(h * ncol, ncol), :] = mass
    copy.wait()
    sum_listed(source, splat, part, lists, 0)
    sums_out[...] = jnp.broadcast_to(pack_sums(part)[None], sums_out.shape)


def target_rows_at(target_rows, n):
    return target_rows[pl.ds(n, NROW, stride=CAP), :]


def take_over(rows, names, wanted, values):
    real = wanted < float(STARS)
    for d in range(CAP):
        rows = jnp.where((turn(names, d) == wanted) & real, turn(values, d), rows)
    return rows


def static_kernel(step, ncol, *refs):
    raw, lists_in, target_rows = refs[:3]
    corrected, refs = refs[3 : 3 + step], refs[3 + step :]
    total_out, splat, targets, lists, sem, source, part = refs
    block_time = (step + 1) * step_size
    copy = pltpu.make_async_copy(lists_in, lists, sem)
    copy.start()
    rows = target_rows_at(target_rows, step)
    wanted = target_rows_at(target_rows, STEPS + step)
    for j in range(step):
        names = target_rows_at(target_rows, STEPS + j)
        rows = take_over(rows, names, wanted, corrected[j][...])
    targets[...] = rows
    spread_targets(rows, splat, block_time)
    predict_sources(raw, source, block_time, ncol)
    masses = load_masses(raw, ncol)
    names = raw[pl.ds(13, ncol, stride=32), :]
    lane = lane_of((ncol, LANES)).astype(jnp.float32)
    for at in range(CAP * step):
        named = jnp.broadcast_to(names[:, at : at + 1], (ncol, LANES))
        for h in range(2):
            masses[h] = jnp.where(named == lane + float(h * LANES), 0.0, masses[h])
    for h in range(2):
        source[6, pl.ds(h * ncol, ncol), :] = masses[h]
    copy.wait()
    sum_listed(source, splat, part, lists, step)
    total_out[...] = pack_sums(part)


def to_columns(x):
    group = lane_of((16, LANES)) // CAP
    row = row_of((16, LANES))
    out = x
    for d in range(16):
        moved = pltpu.roll(x, CAP * d, 1) if d else x
        moved = pltpu.roll(moved, 16 - d, 0) if d else moved
        out = moved if d == 0 else jnp.where(group == (row + d) % 16, moved, out)
    return out


def fresh_kernel(step, ncol, *refs):
    total_in, splat, fresh, *refs = refs
    if step > 1:
        older, *refs = refs
    sums_out, columns, source = refs
    halves = max(ncol // 16, 1)
    blocks = halves * step
    first = halves * (step - 1)
    for h in range(halves):
        columns[pl.ds(16 * (first + h), 16), :] = to_columns(fresh[pl.ds(16 * h, 16), :])
    if step > 1:
        columns[pl.ds(0, 16 * first), :] = older[...]
        for h in range(halves):
            later = columns[pl.ds(16 * (first + h) + 13, 1), :]
            for j in range(step - 1):
                at = 16 * (halves * j + h)
                names = columns[pl.ds(at + 13, 1), :]
                again = jnp.zeros((1, LANES), jnp.float32)
                for d in range(CAP):
                    again = jnp.where(turn(later, d) == names, 1.0, again)
                mass = columns[pl.ds(at + 15, 1), :]
                columns[pl.ds(at + 15, 1), :] = jnp.where(again > 0.5, 0.0, mass)
    for b in range(blocks):
        tau = (step - b // halves) * step_size

        def load(q):
            return columns[pl.ds(16 * b + q, 1), :]

        for c in range(3):
            x, v = predict(load(c), load(3 + c), load(6 + c), load(9 + c), tau)
            source[c, b : b + 1, :] = x
            source[3 + c, b : b + 1, :] = v
        source[6, b : b + 1, :] = load(15)
    lane = lane_of((8, LANES))
    total = total_in[...]
    zero = jnp.zeros((8, LANES), jnp.float32)
    for g in range(GROUPS):
        target = [splat[pl.ds(q * TARGETS + 8 * g, 8), :] for q in range(6)]
        sums = (zero,) * 6
        for b in range(blocks):
            sums = add_pairs(sums, [wide_row(source, q, b) for q in range(7)], target)
        for q in range(6):
            line = jnp.sum(sums[q], axis=1, keepdims=True)
            total = jnp.where(lane == 64 * (g % 2) + CAP * q + g // 2, total + line, total)
    sums_out[...] = jnp.broadcast_to(total[None], sums_out.shape)


def correct(old_acc, old_jerk, new_acc, new_jerk, interval):
    diff = old_acc - new_acc
    interval_sq = interval * interval
    second = (-6.0 * diff - interval * (4.0 * old_jerk + 2.0 * new_jerk)) / interval_sq
    third = (12.0 * diff + 6.0 * interval * (old_jerk + new_jerk)) / (interval_sq * interval)
    pos_step = interval_sq * interval_sq * (second / 24.0 + interval * third / 120.0)
    vel_step = interval_sq * interval * (second / 6.0 + interval * third / 24.0)
    return (pos_step, vel_step)


def correct_rows(step, gathered, target_rows, targets):
    block_time = (step + 1) * step_size
    total = gathered[0]
    for p in range(1, NROW):
        total = total + gathered[p]
    total = jnp.concatenate([total, back(total, 64)], axis=0)
    z = target_rows_at(target_rows, 0) if step == 0 else targets[...]
    names = target_rows_at(target_rows, STEPS + step)
    lane = lane_of((NROW, LANES))
    tau = block_time - back(z, 96)
    old_acc, old_jerk = back(z, 48), back(z, 72)
    x, v = predict(z, back(z, 24), old_acc, old_jerk, tau)
    new_a, new_j = total, back(total, 24)
    pos_step, vel_step = correct(old_acc, old_jerk, new_a, new_j, tau)

    def lay(*parts):
        out = parts[-1]
        for n in reversed(range(len(parts) - 1)):
            piece = pltpu.roll(parts[n], 24 * n, 1) if n else parts[n]
            out = jnp.where(lane < 24 * (n + 1), piece, out)
        return out

    filled = names < float(STARS)
    rest = jnp.where(lane < 120, block_time, z)
    corrected = lay(x + pos_step, v + vel_step, new_a, new_j, rest)
    terms = lay(new_a, new_j, pos_step, vel_step, jnp.zeros_like(z))
    return jnp.where(filled, corrected, 0.0), jnp.where(filled, terms, 0.0), names


def correct_kernel(step, me_of, *refs):
    gathered, target_rows, *refs = refs
    targets = None
    if step > 0:
        targets, *refs = refs
    corrected_out, fresh_out, terms_out, keep = refs
    me = me_of()
    corrected, terms, names = correct_rows(step, gathered, target_rows, targets)
    lane = lane_of((NROW, LANES))
    keep[0] = terms
    terms_out[...] = keep[0, pl.ds(me, 1), :]
    keep[1] = jnp.where((lane >= 104) & (lane < 112), names, corrected)
    fresh_out[...] = jnp.broadcast_to(keep[1, pl.ds(me, 1), :][None], fresh_out.shape)
    corrected_out[...] = corrected


def spread(line):
    diagonal = lane_of((16, LANES)) // CAP == row_of((16, LANES))
    x = jnp.where(diagonal, jnp.broadcast_to(line, (16, LANES)), 0.0)
    for shift in (64, 32, 16, 8):
        x = x + pltpu.roll(x, shift, 1)
    return x


def put(whole, active, step, line):
    columns = spread(line)
    star = lane_of((16, STARS))
    for s in range(CAP):
        whole = jnp.where(star == active[step, s], columns[:, s : s + 1], whole)
    return whole


def slot_terms(line):
    return jnp.transpose(spread(line))[0:CAP, 0:12]


def earlier_steps_kernel(me_of, *refs):
    state, active = refs[:2]
    corrected, terms = refs[2 : STEPS + 1], refs[STEPS + 1 : 2 * STEPS]
    state_out, terms_out = refs[2 * STEPS + 1 :]
    me = me_of()
    whole = state[...]
    for j in range(STEPS - 1):
        whole = put(whole, active, j, corrected[j][pl.ds(me, 1), :])
        terms_out[j] = slot_terms(terms[j][...])
    state_out[...] = whole


def last_kernel(me_of, *refs):
    gathered, target_rows, targets, state, earlier_terms, active = refs[:6]
    new_pos, new_vel, new_acc, new_jerk, terms_out, keep = refs[6:]
    me = me_of()
    corrected, terms, _ = correct_rows(STEPS - 1, gathered, target_rows, targets)
    keep[0] = terms
    keep[1] = corrected
    whole = put(state[...], active, STEPS - 1, keep[1, pl.ds(me, 1), :])
    terms_out[0 : STEPS - 1] = earlier_terms[...]
    terms_out[STEPS - 1] = slot_terms(keep[0, pl.ds(me, 1), :])
    for n, out in enumerate((new_pos, new_vel, new_acc, new_jerk)):
        out[...] = whole[3 * n : 3 * n + 3, :]


def struct(*shape):
    return jax.ShapeDtypeStruct(shape, jnp.float32)


def scratch(*shape):
    return pltpu.VMEM(shape, jnp.float32)


vmem = pl.BlockSpec(memory_space=pltpu.VMEM)
hbm = pl.BlockSpec(memory_space=pltpu.HBM)
smem = pl.BlockSpec(memory_space=pltpu.SMEM)
anywhere = pl.BlockSpec(memory_space=pl.ANY)


def call(kernel, operands, outs, work, specs=None, out_specs=None, flops=None):
    cost = None
    if flops:
        cost = pl.CostEstimate(flops=flops, bytes_accessed=1 << 20, transcendentals=0)
    return pl.pallas_call(
        kernel,
        out_shape=tuple(outs),
        in_specs=specs or [vmem] * len(operands),
        out_specs=out_specs or (vmem,) * len(outs),
        scratch_shapes=work,
        cost_estimate=cost,
        compiler_params=pltpu.CompilerParams(vmem_limit_bytes=8 << 20),
    )(*operands)


def send_all(x, axes):
    return lax.all_to_all(x, axes, split_axis=0, concat_axis=0, tiled=True)


def body(ncol, narrow, pos, vel, acc, jerk, masses, levels, active):
    masses, levels = masses.reshape(1, STARS), levels.reshape(1, STARS)
    pos, vel, acc, jerk, masses, levels, active = (
        pltpu.with_memory_space_constraint(a, pltpu.HBM)
        for a in (pos, vel, acc, jerk, masses, levels, active)
    )
    row_axes = ("core", "narrow")

    def me_of():
        return lax.axis_index("core") * narrow + lax.axis_index("narrow")

    block, rows, state = call(
        pack_kernel,
        (pos, vel, acc, jerk, masses, levels, active),
        (struct(ncol, 32, LANES), struct(NROW, 8, LANES), struct(16, STARS)),
        [scratch(3, STARS)] * 4
        + [scratch(1, STARS), pltpu.VMEM((1, STARS), jnp.int32)]
        + [scratch(32, LANES), scratch(8, LANES), pltpu.SemaphoreType.DMA((6,))],
        [hbm] * 6 + [smem],
    )
    target_rows = send_all(rows, row_axes).reshape(NROW * 8, LANES)
    block, target_rows = lax.optimization_barrier((block, target_rows))
    raw = send_all(block, "across").reshape(ncol * 32, LANES)

    sums_shape = struct(NROW, NROW // 2, LANES)
    source_shape = (7, 2 * ncol, LANES)
    slots = struct(NROW, LANES)
    splat_shape = (6 * TARGETS, LANES)
    list_shape = jax.ShapeDtypeStruct((STEPS, LIST), jnp.int32)
    list_work = [pltpu.SMEM(list_shape.shape, jnp.int32), pltpu.SemaphoreType.DMA]
    sum_work = list_work + [scratch(*source_shape), scratch(*splat_shape)]
    lists, splat = call(
        plan_kernel,
        (target_rows, target_rows),
        (list_shape, struct(*splat_shape)),
        [],
        [smem, vmem],
        (smem, vmem),
        flops=3 * 10**7,
    )
    (sums,) = call(
        functools.partial(first_force_kernel, ncol),
        (raw, lists, splat),
        (sums_shape,),
        sum_work,
        [vmem, anywhere, vmem],
    )
    corrected, terms = [], []
    targets = columns = None
    for step in range(STEPS):
        gathered = send_all(sums, row_axes)
        if step == STEPS - 1:
            break
        operands = [gathered, target_rows] + ([] if step == 0 else [targets])
        done, fresh, own_terms = call(
            functools.partial(correct_kernel, step, me_of),
            operands,
            (slots, struct(ncol, 1, LANES), struct(1, LANES)),
            [scratch(2, NROW, LANES)],
        )
        corrected.append(done)
        terms.append(own_terms)
        fresh = send_all(fresh, "across").reshape(ncol, LANES)
        operands = [raw, lists, target_rows, *corrected]
        static, splat, targets = call(
            functools.partial(static_kernel, step + 1, ncol),
            operands,
            (struct(8, LANES), struct(*splat_shape), slots),
            sum_work,
            [vmem, anywhere] + [vmem] * (step + 2),
            flops=3 * 10**7,
        )
        blocks = max(ncol // 16, 1) * (step + 1)
        operands = [static, splat, fresh] + ([] if step == 0 else [columns])
        outs, work = [sums_shape], [scratch(7, blocks, LANES)]
        if step + 1 < STEPS - 1:
            outs.append(struct(16 * blocks, LANES))
        else:
            work.insert(0, scratch(16 * blocks, LANES))
        sums, *columns = call(
            functools.partial(fresh_kernel, step + 1, ncol), operands, outs, work
        )
        if columns:
            (columns,) = columns
    state, earlier_terms = call(
        functools.partial(earlier_steps_kernel, me_of),
        (state, active, *corrected, *terms, sums),
        (struct(16, STARS), struct(STEPS - 1, CAP, 12)),
        [],
        [vmem, smem] + [vmem] * (2 * STEPS - 2) + [anywhere],
        flops=10**7,
    )
    *new, slot_rows = call(
        functools.partial(last_kernel, me_of),
        (gathered, target_rows, targets, state, earlier_terms, active),
        (struct(3, STARS),) * 4 + (struct(STEPS, CAP, 12),),
        [scratch(2, NROW, LANES)],
        [vmem] * 5 + [smem],
    )
    return (*new, jnp.swapaxes(slot_rows, 1, 2))


def solution(mesh):
    wide, narrow = mesh.shape["wide"], mesh.shape["narrow"]
    ncol = wide // 2
    every = ("across", "core", "narrow")
    finer = Mesh(mesh.devices.reshape(ncol, 2, narrow), every)
    in_specs = (P(None, every),) * 4 + (P(every), P(every), P(None, every))
    out_specs = (P(None, every),) * 4 + (P(None, None, every),)
    return jax.shard_map(
        functools.partial(body, ncol, narrow),
        mesh=finer,
        in_specs=in_specs,
        out_specs=out_specs,
        check_vma=False,
    )
```

```python
import functools

import jax
import jax.numpy as jnp
from jax import lax
from jax.experimental import pallas as pl
from jax.experimental.pallas import tpu as pltpu
from jax.sharding import Mesh, PartitionSpec as P

step_size = 1.0 / 32.0
softening = 2.5e-05
STEPS = 4
CAP = 8
LANES = 128
STARS = 256

NROW = 16
TARGETS = NROW * CAP
GROUPS = TARGETS // 8
AT_ONCE = 8
LIST = TARGETS + 32


def predict(x, v, a, j, tau):
    ahead_x = x + tau * (v + tau * (a * 0.5 + tau * j / 6.0))
    ahead_v = v + tau * (a + tau * j * 0.5)
    return ahead_x, ahead_v


def back(x, lanes):
    return pltpu.roll(x, LANES - lanes, 1) if lanes else x


def lane_of(shape):
    return lax.broadcasted_iota(jnp.int32, shape, 1)


def row_of(shape):
    return lax.broadcasted_iota(jnp.int32, shape, 0)


def turn(x, d):
    if d == 0:
        return x
    slot = lane_of(x.shape) % CAP
    return jnp.where(slot < CAP - d, pltpu.roll(x, LANES - d, 1), pltpu.roll(x, CAP - d, 1))


def fetch(sources, held, sems):
    copies = [pltpu.make_async_copy(a, b, sems.at[n]) for n, (a, b) in enumerate(zip(sources, held))]
    for copy in copies:
        copy.start()
    return copies


def pack_kernel(*refs):
    block_out, row_out, state, *held = refs[7:17]
    block, rows, sems = refs[17:]
    for copy in fetch(refs[:7], held, sems):
        copy.wait()
    pos, vel, acc, jerk, mass, levels, active = held
    for n, part in enumerate((pos, vel, acc, jerk)):
        state[3 * n : 3 * n + 3, :] = part[...]
    times = step_size * (1.0 - jnp.left_shift(1, levels[...]).astype(jnp.float32))
    state[12:15, :] = jnp.broadcast_to(times, (3, STARS))
    state[15:16, :] = mass[...]
    whole = state[...]
    lane = lane_of((1, LANES))
    names = jnp.full((1, LANES), STARS, jnp.int32)
    for k in range(STEPS):
        for s in range(CAP):
            names = jnp.where(lane == CAP * k + s, active[k, s], names)
    block[0:16, :] = whole[:, :LANES]
    block[16:32, :] = whole[:, LANES:]
    block[13:14, :] = names.astype(jnp.float32)
    block_out[...] = jnp.broadcast_to(block[...][None], block_out.shape)
    lane = lane_of((16, LANES))
    diagonal = lane // CAP == row_of((16, LANES))
    slot = lane % CAP
    star = lane_of((1, STARS))
    for k in range(STEPS):
        table = jnp.zeros((16, LANES), jnp.float32)
        names = jnp.zeros((1, LANES), jnp.float32)
        for s in range(CAP):
            named = active[k, s]
            column = jnp.sum(jnp.where(star == named, whole, 0.0), axis=1, keepdims=True)
            table = jnp.where(slot == s, column, table)
            names = jnp.where(slot[0:1] == s, named.astype(jnp.float32), names)
        rows[k : k + 1, :] = jnp.sum(jnp.where(diagonal, table, 0.0), axis=0, keepdims=True)
        rows[STEPS + k : STEPS + k + 1, :] = names
    row_out[...] = jnp.broadcast_to(rows[...][None], row_out.shape)


def plan_kernel(scalars, target_rows, lists, splat):
    for k in range(STEPS):

        def peer(r, n):
            for s in range(CAP):
                lists[k, n] = NROW * s + r
                n = n + jnp.where(scalars[CAP * r + STEPS + k, s] < float(STARS), 1, 0)
            return n

        n = lax.fori_loop(0, NROW, peer, 0)
        for u in range(AT_ONCE):
            lists[k, n + u] = 0
        lists[k, LIST - 1] = n
    spread_targets(target_rows_at(target_rows, 0), splat, step_size)


def predict_sources(raw, source, block_time, ncol):
    for h in range(2):
        at = pl.ds(h * ncol, ncol)

        def load(q):
            return raw[pl.ds(16 * h + q, ncol, stride=32), :]

        tau = block_time - load(12)
        for c in range(3):
            x, v = predict(load(c), load(3 + c), load(6 + c), load(9 + c), tau)
            source[c, at, :] = x
            source[3 + c, at, :] = v


def spread_targets(z, splat, block_time):
    x, v = predict(z, back(z, 24), back(z, 48), back(z, 72), block_time - back(z, 96))
    for q in range(6):
        held = x if q < 3 else v
        for s in range(CAP):
            at = CAP * (q % 3) + s
            splat[pl.ds((q * CAP + s) * NROW, NROW), :] = jnp.broadcast_to(
                held[:, at : at + 1], (NROW, LANES)
            )


def add_pairs(sums, sources, target):
    dx, dy, dz, du, dv, dw = (sources[q] - target[q] for q in range(6))
    radius_sq = (dx * dx + dy * dy + dz * dz) + softening
    inverse = lax.rsqrt(radius_sq)
    inverse_sq = inverse * inverse
    weight = sources[6] * inverse * inverse_sq
    closing = (dx * du + dy * dv + dz * dw) * (3.0 * inverse_sq)
    return (
        sums[0] + weight * dx,
        sums[1] + weight * dy,
        sums[2] + weight * dz,
        sums[3] + weight * (du - closing * dx),
        sums[4] + weight * (dv - closing * dy),
        sums[5] + weight * (dw - closing * dz),
    )


def wide_row(ref, q, r):
    return jnp.broadcast_to(ref[q, pl.ds(r, 1), :], (8, LANES))


def sum_listed(source, splat, part, lists, step):
    chunks = source.shape[1] // 8
    part[...] = jnp.zeros(part.shape, jnp.float32)
    zero = jnp.zeros((8, LANES), jnp.float32)

    def some_targets(n, carry):
        for u in range(AT_ONCE):
            i = lists[step, AT_ONCE * n + u]
            target = [
                jnp.broadcast_to(splat[pl.ds(q * TARGETS + i, 1), :], (8, LANES)) for q in range(6)
            ]
            sums = (zero,) * 6
            for c in range(chunks):
                sums = add_pairs(sums, [source[q, pl.ds(8 * c, 8), :] for q in range(7)], target)
            for q in range(6):
                part[pl.ds(q * TARGETS + i, 1), :] = jnp.sum(sums[q], axis=0, keepdims=True)
        return carry

    lax.fori_loop(0, (lists[step, LIST - 1] + AT_ONCE - 1) // AT_ONCE, some_targets, 0)


def pack_sums(part):
    lane = lane_of((8, LANES))
    total = jnp.zeros((8, LANES), jnp.float32)
    for q in range(6):
        for g in range(GROUPS):
            line = jnp.sum(part[pl.ds(q * TARGETS + 8 * g, 8), :], axis=1, keepdims=True)
            total = jnp.where(lane == 64 * (g % 2) + CAP * q + g // 2, line, total)
    return total


def load_masses(raw, ncol):
    return [raw[pl.ds(16 * h + 15, ncol, stride=32), :] for h in range(2)]


def first_force_kernel(ncol, raw, lists_in, splat, sums_out, lists, sem, source, part):
    copy = pltpu.make_async_copy(lists_in, lists, sem)
    copy.start()
    predict_sources(raw, source, step_size, ncol)
    for h, mass in enumerate(load_masses(raw, ncol)):
        source[6, pl.ds(h * ncol, ncol), :] = mass
    copy.wait()
    sum_listed(source, splat, part, lists, 0)
    sums_out[...] = jnp.broadcast_to(pack_sums(part)[None], sums_out.shape)


def target_rows_at(target_rows, n):
    return target_rows[pl.ds(n, NROW, stride=CAP), :]


def take_over(rows, names, wanted, values):
    real = wanted < float(STARS)
    for d in range(CAP):
        rows = jnp.where((turn(names, d) == wanted) & real, turn(values, d), rows)
    return rows


def static_kernel(step, ncol, *refs):
    raw, lists_in, target_rows = refs[:3]
    corrected, refs = refs[3 : 3 + step], refs[3 + step :]
    total_out, splat, targets, lists, sem, source, part = refs
    block_time = (step + 1) * step_size
    copy = pltpu.make_async_copy(lists_in, lists, sem)
    copy.start()
    rows = target_rows_at(target_rows, step)
    wanted = target_rows_at(target_rows, STEPS + step)
    for j in range(step):
        names = target_rows_at(target_rows, STEPS + j)
        rows = take_over(rows, names, wanted, corrected[j][...])
    targets[...] = rows
    spread_targets(rows, splat, block_time)
    predict_sources(raw, source, block_time, ncol)
    masses = load_masses(raw, ncol)
    names = raw[pl.ds(13, ncol, stride=32), :]
    lane = lane_of((ncol, LANES)).astype(jnp.float32)
    for at in range(CAP * step):
        named = jnp.broadcast_to(names[:, at : at + 1], (ncol, LANES))
        for h in range(2):
            masses[h] = jnp.where(named == lane + float(h * LANES), 0.0, masses[h])
    for h in range(2):
        source[6, pl.ds(h * ncol, ncol), :] = masses[h]
    copy.wait()
    sum_listed(source, splat, part, lists, step)
    total_out[...] = pack_sums(part)


def to_columns(x):
    group = lane_of((16, LANES)) // CAP
    row = row_of((16, LANES))
    out = x
    for d in range(16):
        moved = pltpu.roll(x, CAP * d, 1) if d else x
        moved = pltpu.roll(moved, 16 - d, 0) if d else moved
        out = moved if d == 0 else jnp.where(group == (row + d) % 16, moved, out)
    return out


def fresh_kernel(step, ncol, *refs):
    total_in, splat, fresh, *refs = refs
    if step > 1:
        older, *refs = refs
    sums_out, columns, source = refs
    halves = max(ncol // 16, 1)
    blocks = halves * step
    first = halves * (step - 1)
    for h in range(halves):
        columns[pl.ds(16 * (first + h), 16), :] = to_columns(fresh[pl.ds(16 * h, 16), :])
    if step > 1:
        columns[pl.ds(0, 16 * first), :] = older[...]
        for h in range(halves):
            later = columns[pl.ds(16 * (first + h) + 13, 1), :]
            for j in range(step - 1):
                at = 16 * (halves * j + h)
                names = columns[pl.ds(at + 13, 1), :]
                again = jnp.zeros((1, LANES), jnp.float32)
                for d in range(CAP):
                    again = jnp.where(turn(later, d) == names, 1.0, again)
                mass = columns[pl.ds(at + 15, 1), :]
                columns[pl.ds(at + 15, 1), :] = jnp.where(again > 0.5, 0.0, mass)
    for b in range(blocks):
        tau = (step - b // halves) * step_size

        def load(q):
            return columns[pl.ds(16 * b + q, 1), :]

        for c in range(3):
            x, v = predict(load(c), load(3 + c), load(6 + c), load(9 + c), tau)
            source[c, b : b + 1, :] = x
            source[3 + c, b : b + 1, :] = v
        source[6, b : b + 1, :] = load(15)
    lane = lane_of((8, LANES))
    total = total_in[...]
    zero = jnp.zeros((8, LANES), jnp.float32)
    for g in range(GROUPS):
        target = [splat[pl.ds(q * TARGETS + 8 * g, 8), :] for q in range(6)]
        sums = (zero,) * 6
        for b in range(blocks):
            sums = add_pairs(sums, [wide_row(source, q, b) for q in range(7)], target)
        for q in range(6):
            line = jnp.sum(sums[q], axis=1, keepdims=True)
            total = jnp.where(lane == 64 * (g % 2) + CAP * q + g // 2, total + line, total)
    sums_out[...] = jnp.broadcast_to(total[None], sums_out.shape)


def correct(old_acc, old_jerk, new_acc, new_jerk, interval):
    diff = old_acc - new_acc
    interval_sq = interval * interval
    second = (-6.0 * diff - interval * (4.0 * old_jerk + 2.0 * new_jerk)) / interval_sq
    third = (12.0 * diff + 6.0 * interval * (old_jerk + new_jerk)) / (interval_sq * interval)
    pos_step = interval_sq * interval_sq * (second / 24.0 + interval * third / 120.0)
    vel_step = interval_sq * interval * (second / 6.0 + interval * third / 24.0)
    return (pos_step, vel_step)


def correct_rows(step, gathered, target_rows, targets):
    block_time = (step + 1) * step_size
    total = gathered[0]
    for p in range(1, NROW):
        total = total + gathered[p]
    total = jnp.concatenate([total, back(total, 64)], axis=0)
    z = target_rows_at(target_rows, 0) if step == 0 else targets[...]
    names = target_rows_at(target_rows, STEPS + step)
    lane = lane_of((NROW, LANES))
    tau = block_time - back(z, 96)
    old_acc, old_jerk = back(z, 48), back(z, 72)
    x, v = predict(z, back(z, 24), old_acc, old_jerk, tau)
    new_a, new_j = total, back(total, 24)
    pos_step, vel_step = correct(old_acc, old_jerk, new_a, new_j, tau)

    def lay(*parts):
        out = parts[-1]
        for n in reversed(range(len(parts) - 1)):
            piece = pltpu.roll(parts[n], 24 * n, 1) if n else parts[n]
            out = jnp.where(lane < 24 * (n + 1), piece, out)
        return out

    filled = names < float(STARS)
    rest = jnp.where(lane < 120, block_time, z)
    corrected = lay(x + pos_step, v + vel_step, new_a, new_j, rest)
    terms = lay(new_a, new_j, pos_step, vel_step, jnp.zeros_like(z))
    return jnp.where(filled, corrected, 0.0), jnp.where(filled, terms, 0.0), names


def correct_kernel(step, me_of, *refs):
    gathered, target_rows, *refs = refs
    targets = None
    if step > 0:
        targets, *refs = refs
    corrected_out, fresh_out, terms_out, keep = refs
    me = me_of()
    corrected, terms, names = correct_rows(step, gathered, target_rows, targets)
    lane = lane_of((NROW, LANES))
    keep[0] = terms
    terms_out[...] = keep[0, pl.ds(me, 1), :]
    keep[1] = jnp.where((lane >= 104) & (lane < 112), names, corrected)
    fresh_out[...] = jnp.broadcast_to(keep[1, pl.ds(me, 1), :][None], fresh_out.shape)
    corrected_out[...] = corrected


def spread(line):
    diagonal = lane_of((16, LANES)) // CAP == row_of((16, LANES))
    x = jnp.where(diagonal, jnp.broadcast_to(line, (16, LANES)), 0.0)
    for shift in (64, 32, 16, 8):
        x = x + pltpu.roll(x, shift, 1)
    return x


def put(whole, names, line):
    columns = spread(line)
    star = lane_of((16, STARS)).astype(jnp.float32)
    for s in range(CAP):
        whole = jnp.where(star == names[:, s : s + 1], columns[:, s : s + 1], whole)
    return whole


def slot_terms(line):
    return jnp.transpose(spread(line))[0:CAP, 0:12]


def last_kernel(me_of, *refs):
    gathered, target_rows, targets, state = refs[:4]
    corrected, terms = refs[4 : STEPS + 3], refs[STEPS + 3 : 2 * STEPS + 2]
    new_pos, new_vel, new_acc, new_jerk, terms_out, keep = refs[2 * STEPS + 2 :]
    me = me_of()
    last_corrected, last_terms, _ = correct_rows(STEPS - 1, gathered, target_rows, targets)
    keep[0] = last_terms
    keep[1] = last_corrected
    whole = state[...]
    for j in range(STEPS):
        names = target_rows[pl.ds(CAP * me + STEPS + j, 1), :]
        last = j == STEPS - 1
        line = keep[1, pl.ds(me, 1), :] if last else corrected[j][pl.ds(me, 1), :]
        whole = put(whole, names, line)
        terms_out[j] = slot_terms(keep[0, pl.ds(me, 1), :] if last else terms[j][...])
    for n, out in enumerate((new_pos, new_vel, new_acc, new_jerk)):
        out[...] = whole[3 * n : 3 * n + 3, :]


def struct(*shape):
    return jax.ShapeDtypeStruct(shape, jnp.float32)


def scratch(*shape):
    return pltpu.VMEM(shape, jnp.float32)


vmem = pl.BlockSpec(memory_space=pltpu.VMEM)
hbm = pl.BlockSpec(memory_space=pltpu.HBM)
smem = pl.BlockSpec(memory_space=pltpu.SMEM)
anywhere = pl.BlockSpec(memory_space=pl.ANY)


def call(kernel, operands, outs, work, specs=None, out_specs=None, flops=None):
    cost = None
    if flops:
        cost = pl.CostEstimate(flops=flops, bytes_accessed=1 << 20, transcendentals=0)
    return pl.pallas_call(
        kernel,
        out_shape=tuple(outs),
        in_specs=specs or [vmem] * len(operands),
        out_specs=out_specs or (vmem,) * len(outs),
        scratch_shapes=work,
        cost_estimate=cost,
        compiler_params=pltpu.CompilerParams(vmem_limit_bytes=8 << 20),
    )(*operands)


def send_all(x, axes):
    return lax.all_to_all(x, axes, split_axis=0, concat_axis=0, tiled=True)


def body(ncol, narrow, pos, vel, acc, jerk, masses, levels, active):
    masses, levels = masses.reshape(1, STARS), levels.reshape(1, STARS)
    pos, vel, acc, jerk, masses, levels, active = (
        pltpu.with_memory_space_constraint(a, pltpu.HBM)
        for a in (pos, vel, acc, jerk, masses, levels, active)
    )
    row_axes = ("core", "narrow")

    def me_of():
        return lax.axis_index("core") * narrow + lax.axis_index("narrow")

    block, rows, state = call(
        pack_kernel,
        (pos, vel, acc, jerk, masses, levels, active),
        (struct(ncol, 32, LANES), struct(NROW, 8, LANES), struct(16, STARS)),
        [scratch(3, STARS)] * 4
        + [scratch(1, STARS), pltpu.VMEM((1, STARS), jnp.int32)]
        + [pltpu.SMEM((STEPS, CAP), jnp.int32)]
        + [scratch(32, LANES), scratch(8, LANES), pltpu.SemaphoreType.DMA((7,))],
        [hbm] * 7,
    )
    target_rows = send_all(rows, row_axes).reshape(NROW * 8, LANES)
    block, target_rows = lax.optimization_barrier((block, target_rows))
    raw = send_all(block, "across").reshape(ncol * 32, LANES)

    sums_shape = struct(NROW, NROW // 2, LANES)
    source_shape = (7, 2 * ncol, LANES)
    slots = struct(NROW, LANES)
    splat_shape = (6 * TARGETS, LANES)
    list_shape = jax.ShapeDtypeStruct((STEPS, LIST), jnp.int32)
    list_work = [pltpu.SMEM(list_shape.shape, jnp.int32), pltpu.SemaphoreType.DMA]
    sum_work = list_work + [scratch(*source_shape), scratch(*splat_shape)]
    lists, splat = call(
        plan_kernel,
        (target_rows, target_rows),
        (list_shape, struct(*splat_shape)),
        [],
        [smem, vmem],
        (smem, vmem),
        flops=3 * 10**7,
    )
    (sums,) = call(
        functools.partial(first_force_kernel, ncol),
        (raw, lists, splat),
        (sums_shape,),
        sum_work,
        [vmem, anywhere, vmem],
    )
    corrected, terms = [], []
    targets = columns = None
    for step in range(STEPS):
        gathered = send_all(sums, row_axes)
        if step == STEPS - 1:
            break
        operands = [gathered, target_rows] + ([] if step == 0 else [targets])
        done, fresh, own_terms = call(
            functools.partial(correct_kernel, step, me_of),
            operands,
            (slots, struct(ncol, 1, LANES), struct(1, LANES)),
            [scratch(2, NROW, LANES)],
        )
        corrected.append(done)
        terms.append(own_terms)
        fresh = send_all(fresh, "across").reshape(ncol, LANES)
        operands = [raw, lists, target_rows, *corrected]
        static, splat, targets = call(
            functools.partial(static_kernel, step + 1, ncol),
            operands,
            (struct(8, LANES), struct(*splat_shape), slots),
            sum_work,
            [vmem, anywhere] + [vmem] * (step + 2),
            flops=3 * 10**7,
        )
        blocks = max(ncol // 16, 1) * (step + 1)
        operands = [static, splat, fresh] + ([] if step == 0 else [columns])
        outs, work = [sums_shape], [scratch(7, blocks, LANES)]
        if step + 1 < STEPS - 1:
            outs.append(struct(16 * blocks, LANES))
        else:
            work.insert(0, scratch(16 * blocks, LANES))
        sums, *columns = call(
            functools.partial(fresh_kernel, step + 1, ncol), operands, outs, work
        )
        if columns:
            (columns,) = columns
    *new, slot_rows = call(
        functools.partial(last_kernel, me_of),
        (gathered, target_rows, targets, state, *corrected, *terms),
        (struct(3, STARS),) * 4 + (struct(STEPS, CAP, 12),),
        [scratch(2, NROW, LANES)],
    )
    return (*new, jnp.swapaxes(slot_rows, 1, 2))


def solution(mesh):
    wide, narrow = mesh.shape["wide"], mesh.shape["narrow"]
    ncol = wide // 2
    every = ("across", "core", "narrow")
    finer = Mesh(mesh.devices.reshape(ncol, 2, narrow), every)
    in_specs = (P(None, every),) * 4 + (P(every), P(every), P(None, every))
    out_specs = (P(None, every),) * 4 + (P(None, None, every),)
    return jax.shard_map(
        functools.partial(body, ncol, narrow),
        mesh=finer,
        in_specs=in_specs,
        out_specs=out_specs,
        check_vma=False,
    )
```

```python
import functools

import jax
import jax.numpy as jnp
from jax import lax
from jax.experimental import pallas as pl
from jax.experimental.pallas import tpu as pltpu
from jax.sharding import Mesh, PartitionSpec as P

step_size = 1.0 / 32.0
softening = 2.5e-05
STEPS = 4
CAP = 8
LANES = 128
STARS = 256

NROW = 16
TARGETS = NROW * CAP
GROUPS = TARGETS // 8
AT_ONCE = 8
LIST = TARGETS + 32


def predict(x, v, a, j, tau):
    ahead_x = x + tau * (v + tau * (a * 0.5 + tau * j / 6.0))
    ahead_v = v + tau * (a + tau * j * 0.5)
    return ahead_x, ahead_v


def back(x, lanes):
    return pltpu.roll(x, LANES - lanes, 1) if lanes else x


def lane_of(shape):
    return lax.broadcasted_iota(jnp.int32, shape, 1)


def row_of(shape):
    return lax.broadcasted_iota(jnp.int32, shape, 0)


def turn(x, d):
    if d == 0:
        return x
    slot = lane_of(x.shape) % CAP
    return jnp.where(slot < CAP - d, pltpu.roll(x, LANES - d, 1), pltpu.roll(x, CAP - d, 1))


def fetch(sources, held, sems):
    copies = [pltpu.make_async_copy(a, b, sems.at[n]) for n, (a, b) in enumerate(zip(sources, held))]
    for copy in copies:
        copy.start()
    return copies


def pack_kernel(*refs):
    block_out, row_out, state, *held = refs[7:17]
    block, rows, sems = refs[17:]
    for copy in fetch(refs[:7], held, sems):
        copy.wait()
    pos, vel, acc, jerk, mass, levels, active = held
    for n, part in enumerate((pos, vel, acc, jerk)):
        state[3 * n : 3 * n + 3, :] = part[...]
    times = step_size * (1.0 - jnp.left_shift(1, levels[...]).astype(jnp.float32))
    state[12:15, :] = jnp.broadcast_to(times, (3, STARS))
    state[15:16, :] = mass[...]
    whole = state[...]
    lane = lane_of((1, LANES))
    names = jnp.full((1, LANES), STARS, jnp.int32)
    for k in range(STEPS):
        for s in range(CAP):
            names = jnp.where(lane == CAP * k + s, active[k, s], names)
    block[0:16, :] = whole[:, :LANES]
    block[16:32, :] = whole[:, LANES:]
    block[13:14, :] = names.astype(jnp.float32)
    block_out[...] = jnp.broadcast_to(block[...][None], block_out.shape)
    lane = lane_of((16, LANES))
    diagonal = lane // CAP == row_of((16, LANES))
    slot = lane % CAP
    star = lane_of((1, STARS))
    for k in range(STEPS):
        table = jnp.zeros((16, LANES), jnp.float32)
        names = jnp.zeros((1, LANES), jnp.float32)
        for s in range(CAP):
            named = active[k, s]
            column = jnp.sum(jnp.where(star == named, whole, 0.0), axis=1, keepdims=True)
            table = jnp.where(slot == s, column, table)
            names = jnp.where(slot[0:1] == s, named.astype(jnp.float32), names)
        rows[k : k + 1, :] = jnp.sum(jnp.where(diagonal, table, 0.0), axis=0, keepdims=True)
        rows[STEPS + k : STEPS + k + 1, :] = names
    row_out[...] = jnp.broadcast_to(rows[...][None], row_out.shape)


class Plan:
    def __init__(self, target_rows, step, counts, scalars, sem, lists):
        self.scalars, self.lists = scalars, lists
        names = target_rows_at(target_rows, STEPS + step)
        lane = lane_of((NROW, LANES))
        named = jnp.where((names < float(STARS)) & (lane < CAP), 1.0, 0.0)
        count = jnp.sum(named, axis=1, keepdims=True)
        count = jnp.where(lane == row_of((NROW, LANES)), count, 0.0)
        count = jnp.sum(count, axis=0, keepdims=True).astype(jnp.int32)
        counts[...] = jnp.broadcast_to(count, (8, LANES))
        self.copy = pltpu.make_async_copy(counts, scalars, sem)
        self.copy.start()

    def make(self):
        self.copy.wait()
        n = 0
        for r in range(NROW):
            for s in range(CAP):
                self.lists[n + s] = NROW * s + r
            n = n + self.scalars[0, r]
        for u in range(AT_ONCE):
            self.lists[n + u] = 0
        return n


def predict_sources(raw, source, block_time, ncol):
    for h in range(2):
        at = pl.ds(h * ncol, ncol)

        def load(q):
            return raw[pl.ds(16 * h + q, ncol, stride=32), :]

        tau = block_time - load(12)
        for c in range(3):
            x, v = predict(load(c), load(3 + c), load(6 + c), load(9 + c), tau)
            source[c, at, :] = x
            source[3 + c, at, :] = v


def spread_targets(z, splat, block_time):
    x, v = predict(z, back(z, 24), back(z, 48), back(z, 72), block_time - back(z, 96))
    for q in range(6):
        held = x if q < 3 else v
        for s in range(CAP):
            at = CAP * (q % 3) + s
            splat[pl.ds((q * CAP + s) * NROW, NROW), :] = jnp.broadcast_to(
                held[:, at : at + 1], (NROW, LANES)
            )


def add_pairs(sums, sources, target):
    dx, dy, dz, du, dv, dw = (sources[q] - target[q] for q in range(6))
    radius_sq = (dx * dx + dy * dy + dz * dz) + softening
    inverse = lax.rsqrt(radius_sq)
    inverse_sq = inverse * inverse
    weight = sources[6] * inverse * inverse_sq
    closing = (dx * du + dy * dv + dz * dw) * inverse_sq
    fx, fy, fz = weight * dx, weight * dy, weight * dz
    return (
        sums[0] + fx,
        sums[1] + fy,
        sums[2] + fz,
        sums[3] + weight * du,
        sums[4] + weight * dv,
        sums[5] + weight * dw,
        sums[6] + closing * fx,
        sums[7] + closing * fy,
        sums[8] + closing * fz,
    )


def force_and_jerk(sums):
    return [*sums[:3], *(sums[n] - 3.0 * sums[n + 3] for n in range(3, 6))]


def wide_row(ref, q, r):
    return jnp.broadcast_to(ref[q, pl.ds(r, 1), :], (8, LANES))


def sum_listed(source, splat, part, plan):
    count = plan.make()
    chunks = source.shape[1] // 8
    part[...] = jnp.zeros(part.shape, jnp.float32)
    zero = jnp.zeros((8, LANES), jnp.float32)

    def some_targets(n, carry):
        for u in range(AT_ONCE):
            i = plan.lists[AT_ONCE * n + u]
            target = [
                jnp.broadcast_to(splat[pl.ds(q * TARGETS + i, 1), :], (8, LANES)) for q in range(6)
            ]
            sums = (zero,) * 9
            for c in range(chunks):
                sums = add_pairs(sums, [source[q, pl.ds(8 * c, 8), :] for q in range(7)], target)
            sums = force_and_jerk(sums)
            for q in range(6):
                part[pl.ds(q * TARGETS + i, 1), :] = jnp.sum(sums[q], axis=0, keepdims=True)
        return carry

    lax.fori_loop(0, (count + AT_ONCE - 1) // AT_ONCE, some_targets, 0)


def pack_sums(part):
    lane = lane_of((8, LANES))
    total = jnp.zeros((8, LANES), jnp.float32)
    for q in range(6):
        for g in range(GROUPS):
            line = jnp.sum(part[pl.ds(q * TARGETS + 8 * g, 8), :], axis=1, keepdims=True)
            total = jnp.where(lane == 64 * (g % 2) + CAP * q + g // 2, line, total)
    return total


def load_masses(raw, ncol):
    return [raw[pl.ds(16 * h + 15, ncol, stride=32), :] for h in range(2)]


def first_force_kernel(ncol, raw, target_rows, sums_out, *work):
    *plan_work, source, splat, part = work
    plan = Plan(target_rows, 0, *plan_work)
    predict_sources(raw, source, step_size, ncol)
    for h, mass in enumerate(load_masses(raw, ncol)):
        source[6, pl.ds(h * ncol, ncol), :] = mass
    spread_targets(target_rows_at(target_rows, 0), splat, step_size)
    sum_listed(source, splat, part, plan)
    sums_out[...] = jnp.broadcast_to(pack_sums(part)[None], sums_out.shape)


def target_rows_at(target_rows, n):
    return target_rows[pl.ds(n, NROW, stride=CAP), :]


def take_over(rows, names, wanted, values):
    real = wanted < float(STARS)
    for d in range(CAP):
        rows = jnp.where((turn(names, d) == wanted) & real, turn(values, d), rows)
    return rows


def static_kernel(step, ncol, *refs):
    raw, target_rows = refs[:2]
    corrected, refs = refs[2 : 2 + step], refs[2 + step :]
    total_out, splat, targets, *plan_work, source, part = refs
    block_time = (step + 1) * step_size
    plan = Plan(target_rows, step, *plan_work)
    rows = target_rows_at(target_rows, step)
    wanted = target_rows_at(target_rows, STEPS + step)
    for j in range(step):
        names = target_rows_at(target_rows, STEPS + j)
        rows = take_over(rows, names, wanted, corrected[j][...])
    targets[...] = rows
    spread_targets(rows, splat, block_time)
    predict_sources(raw, source, block_time, ncol)
    masses = load_masses(raw, ncol)
    names = raw[pl.ds(13, ncol, stride=32), :]
    lane = lane_of((ncol, LANES)).astype(jnp.float32)
    for at in range(CAP * step):
        named = jnp.broadcast_to(names[:, at : at + 1], (ncol, LANES))
        for h in range(2):
            masses[h] = jnp.where(named == lane + float(h * LANES), 0.0, masses[h])
    for h in range(2):
        source[6, pl.ds(h * ncol, ncol), :] = masses[h]
    sum_listed(source, splat, part, plan)
    total_out[...] = pack_sums(part)


def to_columns(x):
    group = lane_of((16, LANES)) // CAP
    row = row_of((16, LANES))
    out = x
    for d in range(16):
        moved = pltpu.roll(x, CAP * d, 1) if d else x
        moved = pltpu.roll(moved, 16 - d, 0) if d else moved
        out = moved if d == 0 else jnp.where(group == (row + d) % 16, moved, out)
    return out


def fresh_kernel(step, ncol, *refs):
    total_in, splat, fresh, *refs = refs
    if step > 1:
        older, *refs = refs
    sums_out, columns, source = refs
    halves = max(ncol // 16, 1)
    blocks = halves * step
    first = halves * (step - 1)
    for h in range(halves):
        columns[pl.ds(16 * (first + h), 16), :] = to_columns(fresh[pl.ds(16 * h, 16), :])
    if step > 1:
        columns[pl.ds(0, 16 * first), :] = older[...]
        for h in range(halves):
            later = columns[pl.ds(16 * (first + h) + 13, 1), :]
            for j in range(step - 1):
                at = 16 * (halves * j + h)
                names = columns[pl.ds(at + 13, 1), :]
                again = jnp.zeros((1, LANES), jnp.float32)
                for d in range(CAP):
                    again = jnp.where(turn(later, d) == names, 1.0, again)
                mass = columns[pl.ds(at + 15, 1), :]
                columns[pl.ds(at + 15, 1), :] = jnp.where(again > 0.5, 0.0, mass)
    for b in range(blocks):
        tau = (step - b // halves) * step_size

        def load(q):
            return columns[pl.ds(16 * b + q, 1), :]

        for c in range(3):
            x, v = predict(load(c), load(3 + c), load(6 + c), load(9 + c), tau)
            source[c, b : b + 1, :] = x
            source[3 + c, b : b + 1, :] = v
        source[6, b : b + 1, :] = load(15)
    lane = lane_of((8, LANES))
    total = total_in[...]
    zero = jnp.zeros((8, LANES), jnp.float32)
    for g in range(GROUPS):
        target = [splat[pl.ds(q * TARGETS + 8 * g, 8), :] for q in range(6)]
        sums = (zero,) * 9
        for b in range(blocks):
            sums = add_pairs(sums, [wide_row(source, q, b) for q in range(7)], target)
        sums = force_and_jerk(sums)
        for q in range(6):
            line = jnp.sum(sums[q], axis=1, keepdims=True)
            total = jnp.where(lane == 64 * (g % 2) + CAP * q + g // 2, total + line, total)
    if step == STEPS - 1:
        upper = back(total, 64)
        for r in range(CAP):
            sums_out[r] = total[r : r + 1]
            sums_out[CAP + r] = upper[r : r + 1]
    else:
        sums_out[...] = jnp.broadcast_to(total[None], sums_out.shape)


def correct(old_acc, old_jerk, new_acc, new_jerk, interval):
    diff = old_acc - new_acc
    interval_sq = interval * interval
    second = (-6.0 * diff - interval * (4.0 * old_jerk + 2.0 * new_jerk)) / interval_sq
    third = (12.0 * diff + 6.0 * interval * (old_jerk + new_jerk)) / (interval_sq * interval)
    pos_step = interval_sq * interval_sq * (second / 24.0 + interval * third / 120.0)
    vel_step = interval_sq * interval * (second / 6.0 + interval * third / 24.0)
    return (pos_step, vel_step)


def add_peers(gathered):
    total = gathered[0]
    for p in range(1, NROW):
        total = total + gathered[p]
    return jnp.concatenate([total, back(total, 64)], axis=0)


def correct_rows(step, total, z, names):
    block_time = (step + 1) * step_size
    lane = lane_of(z.shape)
    tau = block_time - back(z, 96)
    old_acc, old_jerk = back(z, 48), back(z, 72)
    x, v = predict(z, back(z, 24), old_acc, old_jerk, tau)
    new_a, new_j = total, back(total, 24)
    pos_step, vel_step = correct(old_acc, old_jerk, new_a, new_j, tau)

    def lay(*parts):
        out = parts[-1]
        for n in reversed(range(len(parts) - 1)):
            piece = pltpu.roll(parts[n], 24 * n, 1) if n else parts[n]
            out = jnp.where(lane < 24 * (n + 1), piece, out)
        return out

    filled = names < float(STARS)
    rest = jnp.where(lane < 120, block_time, z)
    corrected = lay(x + pos_step, v + vel_step, new_a, new_j, rest)
    terms = lay(new_a, new_j, pos_step, vel_step, jnp.zeros_like(z))
    return jnp.where(filled, corrected, 0.0), jnp.where(filled, terms, 0.0)


def correct_kernel(step, me_of, *refs):
    gathered, target_rows, *refs = refs
    targets = None
    if step > 0:
        targets, *refs = refs
    corrected_out, fresh_out, terms_out, keep = refs
    me = me_of()
    z = target_rows_at(target_rows, 0) if step == 0 else targets[...]
    names = target_rows_at(target_rows, STEPS + step)
    corrected, terms = correct_rows(step, add_peers(gathered), z, names)
    lane = lane_of((NROW, LANES))
    keep[0] = terms
    terms_out[...] = keep[0, pl.ds(me, 1), :]
    keep[1] = jnp.where((lane >= 104) & (lane < 112), names, corrected)
    fresh_out[...] = jnp.broadcast_to(keep[1, pl.ds(me, 1), :][None], fresh_out.shape)
    corrected_out[...] = corrected


def spread(line):
    diagonal = lane_of((16, LANES)) // CAP == row_of((16, LANES))
    x = jnp.where(diagonal, jnp.broadcast_to(line, (16, LANES)), 0.0)
    for shift in (64, 32, 16, 8):
        x = x + pltpu.roll(x, shift, 1)
    return x


def put(whole, names, line):
    columns = spread(line)
    star = lane_of((16, STARS)).astype(jnp.float32)
    for s in range(CAP):
        whole = jnp.where(star == names[:, s : s + 1], columns[:, s : s + 1], whole)
    return whole


def slot_terms(line):
    return jnp.transpose(spread(line))[0:CAP, 0:12]


def last_kernel(me_of, *refs):
    gathered, target_rows, targets, state = refs[:4]
    corrected, terms = refs[4 : STEPS + 3], refs[STEPS + 3 : 2 * STEPS + 2]
    new_pos, new_vel, new_acc, new_jerk, terms_out = refs[2 * STEPS + 2 :]
    me = me_of()
    names = [target_rows[pl.ds(CAP * me + STEPS + j, 1), :] for j in range(STEPS)]
    total = jnp.sum(gathered[...], axis=0, keepdims=True)
    own, own_terms = correct_rows(STEPS - 1, total, targets[pl.ds(me, 1), :], names[-1])
    whole = state[...]
    for j in range(STEPS):
        last = j == STEPS - 1
        whole = put(whole, names[j], own if last else corrected[j][pl.ds(me, 1), :])
        terms_out[j] = slot_terms(own_terms if last else terms[j][...])
    for n, out in enumerate((new_pos, new_vel, new_acc, new_jerk)):
        out[...] = whole[3 * n : 3 * n + 3, :]


def struct(*shape):
    return jax.ShapeDtypeStruct(shape, jnp.float32)


def scratch(*shape):
    return pltpu.VMEM(shape, jnp.float32)


vmem = pl.BlockSpec(memory_space=pltpu.VMEM)
hbm = pl.BlockSpec(memory_space=pltpu.HBM)
smem = pl.BlockSpec(memory_space=pltpu.SMEM)
anywhere = pl.BlockSpec(memory_space=pl.ANY)


def call(kernel, operands, outs, work, specs=None, out_specs=None, flops=None):
    cost = None
    if flops:
        cost = pl.CostEstimate(flops=flops, bytes_accessed=1 << 20, transcendentals=0)
    return pl.pallas_call(
        kernel,
        out_shape=tuple(outs),
        in_specs=specs or [vmem] * len(operands),
        out_specs=out_specs or (vmem,) * len(outs),
        scratch_shapes=work,
        cost_estimate=cost,
        compiler_params=pltpu.CompilerParams(vmem_limit_bytes=8 << 20),
    )(*operands)


def send_all(x, axes):
    return lax.all_to_all(x, axes, split_axis=0, concat_axis=0, tiled=True)


def body(ncol, narrow, pos, vel, acc, jerk, masses, levels, active):
    masses, levels = masses.reshape(1, STARS), levels.reshape(1, STARS)
    pos, vel, acc, jerk, masses, levels, active = (
        pltpu.with_memory_space_constraint(a, pltpu.HBM)
        for a in (pos, vel, acc, jerk, masses, levels, active)
    )
    row_axes = ("core", "narrow")

    def me_of():
        return lax.axis_index("core") * narrow + lax.axis_index("narrow")

    block, rows, state = call(
        pack_kernel,
        (pos, vel, acc, jerk, masses, levels, active),
        (struct(ncol, 32, LANES), struct(NROW, 8, LANES), struct(16, STARS)),
        [scratch(3, STARS)] * 4
        + [scratch(1, STARS), pltpu.VMEM((1, STARS), jnp.int32)]
        + [pltpu.SMEM((STEPS, CAP), jnp.int32)]
        + [scratch(32, LANES), scratch(8, LANES), pltpu.SemaphoreType.DMA((7,))],
        [hbm] * 7,
    )
    target_rows = send_all(rows, row_axes).reshape(NROW * 8, LANES)
    block, target_rows = lax.optimization_barrier((block, target_rows))
    raw = send_all(block, "across").reshape(ncol * 32, LANES)

    sums_shape = struct(NROW, NROW // 2, LANES)
    source_shape = (7, 2 * ncol, LANES)
    slots = struct(NROW, LANES)
    splat_shape = (6 * TARGETS, LANES)
    plan_work = [
        pltpu.VMEM((8, LANES), jnp.int32),
        pltpu.SMEM((8, LANES), jnp.int32),
        pltpu.SemaphoreType.DMA,
        pltpu.SMEM((LIST,), jnp.int32),
    ]
    source_work, splat_work = scratch(*source_shape), scratch(*splat_shape)
    (sums,) = call(
        functools.partial(first_force_kernel, ncol),
        (raw, target_rows),
        (sums_shape,),
        [*plan_work, source_work, splat_work, splat_work],
    )
    corrected, terms = [], []
    targets = columns = None
    for step in range(STEPS):
        gathered = send_all(sums, row_axes)
        if step == STEPS - 1:
            break
        operands = [gathered, target_rows] + ([] if step == 0 else [targets])
        done, fresh, own_terms = call(
            functools.partial(correct_kernel, step, me_of),
            operands,
            (slots, struct(ncol, 1, LANES), struct(1, LANES)),
            [scratch(2, NROW, LANES)],
        )
        corrected.append(done)
        terms.append(own_terms)
        fresh = send_all(fresh, "across").reshape(ncol, LANES)
        static, splat, targets = call(
            functools.partial(static_kernel, step + 1, ncol),
            (raw, target_rows, *corrected),
            (struct(8, LANES), struct(*splat_shape), slots),
            [*plan_work, source_work, splat_work],
            flops=3 * 10**7,
        )
        blocks = max(ncol // 16, 1) * (step + 1)
        operands = [static, splat, fresh] + ([] if step == 0 else [columns])
        outs, work = [sums_shape], [scratch(7, blocks, LANES)]
        if step + 1 < STEPS - 1:
            outs.append(struct(16 * blocks, LANES))
        else:
            outs[0] = struct(NROW, 1, LANES)
            work.insert(0, scratch(16 * blocks, LANES))
        sums, *columns = call(
            functools.partial(fresh_kernel, step + 1, ncol), operands, outs, work
        )
        if columns:
            (columns,) = columns
    *new, slot_rows = call(
        functools.partial(last_kernel, me_of),
        (gathered.reshape(NROW, LANES), target_rows, targets, state, *corrected, *terms),
        (struct(3, STARS),) * 4 + (struct(STEPS, CAP, 12),),
        [],
    )
    return (*new, jnp.swapaxes(slot_rows, 1, 2))


def solution(mesh):
    wide, narrow = mesh.shape["wide"], mesh.shape["narrow"]
    ncol = wide // 2
    every = ("across", "core", "narrow")
    finer = Mesh(mesh.devices.reshape(ncol, 2, narrow), every)
    in_specs = (P(None, every),) * 4 + (P(every), P(every), P(None, every))
    out_specs = (P(None, every),) * 4 + (P(None, None, every),)
    return jax.shard_map(
        functools.partial(body, ncol, narrow),
        mesh=finer,
        in_specs=in_specs,
        out_specs=out_specs,
        check_vma=False,
    )
```

```python
import functools
import math

import jax
import jax.numpy as jnp
from jax import lax
from jax.experimental import pallas as pl
from jax.experimental.pallas import tpu as pltpu
from jax.sharding import Mesh, PartitionSpec as P

step_size = 1.0 / 32.0
softening = 2.5e-05
STEPS = 4
CAP = 8
LANES = 128
STARS = 256

NROW = 16
TARGETS = NROW * CAP
GROUPS = TARGETS // 8
AT_ONCE = 8
LIST = TARGETS + 32


def predict(x, v, a, j, tau):
    ahead_x = x + tau * (v + tau * (a * 0.5 + tau * j / 6.0))
    ahead_v = v + tau * (a + tau * j * 0.5)
    return ahead_x, ahead_v


def back(x, lanes):
    return pltpu.roll(x, LANES - lanes, 1) if lanes else x


def lane_of(shape):
    return lax.broadcasted_iota(jnp.int32, shape, 1)


def row_of(shape):
    return lax.broadcasted_iota(jnp.int32, shape, 0)


def turn(x, d):
    if d == 0:
        return x
    slot = lane_of(x.shape) % CAP
    return jnp.where(slot < CAP - d, pltpu.roll(x, LANES - d, 1), pltpu.roll(x, CAP - d, 1))


def fetch(sources, held, sems):
    copies = [pltpu.make_async_copy(a, b, sems.at[n]) for n, (a, b) in enumerate(zip(sources, held))]
    for copy in copies:
        copy.start()
    return copies


def pack_kernel(*refs):
    block_out, row_out, state, *held = refs[7:17]
    block, rows, sems = refs[17:]
    for copy in fetch(refs[:7], held, sems):
        copy.wait()
    pos, vel, acc, jerk, mass, levels, active = held
    for n, part in enumerate((pos, vel, acc, jerk)):
        state[3 * n : 3 * n + 3, :] = part[...]
    times = step_size * (1.0 - jnp.left_shift(1, levels[...]).astype(jnp.float32))
    state[12:15, :] = jnp.broadcast_to(times, (3, STARS))
    state[15:16, :] = mass[...]
    whole = state[...]
    lane = lane_of((1, LANES))
    names = jnp.full((1, LANES), STARS, jnp.int32)
    for k in range(STEPS):
        for s in range(CAP):
            names = jnp.where(lane == CAP * k + s, active[k, s], names)
    block[0:16, :] = whole[:, :LANES]
    block[16:32, :] = whole[:, LANES:]
    block[13:14, :] = names.astype(jnp.float32)
    block_out[...] = jnp.broadcast_to(block[...][None], block_out.shape)
    lane = lane_of((16, LANES))
    diagonal = lane // CAP == row_of((16, LANES))
    slot = lane % CAP
    star = lane_of((1, STARS))
    for k in range(STEPS):
        table = jnp.zeros((16, LANES), jnp.float32)
        names = jnp.zeros((1, LANES), jnp.float32)
        for s in range(CAP):
            named = active[k, s]
            column = jnp.sum(jnp.where(star == named, whole, 0.0), axis=1, keepdims=True)
            table = jnp.where(slot == s, column, table)
            names = jnp.where(slot[0:1] == s, named.astype(jnp.float32), names)
        rows[k : k + 1, :] = jnp.sum(jnp.where(diagonal, table, 0.0), axis=0, keepdims=True)
        rows[STEPS + k : STEPS + k + 1, :] = names
    row_out[...] = jnp.broadcast_to(rows[...][None], row_out.shape)


class Plan:
    def __init__(self, target_rows, step, counts, scalars, sem, lists):
        self.scalars, self.lists = scalars, lists
        names = target_rows_at(target_rows, STEPS + step)
        lane = lane_of((NROW, LANES))
        named = jnp.where((names < float(STARS)) & (lane < CAP), 1.0, 0.0)
        count = jnp.sum(named, axis=1, keepdims=True)
        count = jnp.where(lane == row_of((NROW, LANES)), count, 0.0)
        count = jnp.sum(count, axis=0, keepdims=True).astype(jnp.int32)
        counts[...] = jnp.broadcast_to(count, (8, LANES))
        self.copy = pltpu.make_async_copy(counts, scalars, sem)
        self.copy.start()

    def make(self):
        self.copy.wait()
        n = 0
        for r in range(NROW):
            for s in range(CAP):
                self.lists[n + s] = NROW * s + r
            n = n + self.scalars[0, r]
        for u in range(AT_ONCE):
            self.lists[n + u] = 0
        return n


def predict_sources(raw, source, block_time, ncol):
    for h in range(2):
        at = pl.ds(h * ncol, ncol)

        def load(q):
            return raw[pl.ds(16 * h + q, ncol, stride=32), :]

        tau = block_time - load(12)
        for c in range(3):
            x, v = predict(load(c), load(3 + c), load(6 + c), load(9 + c), tau)
            source[c, at, :] = x
            source[3 + c, at, :] = v


def spread_targets(z, splat, block_time):
    x, v = predict(z, back(z, 24), back(z, 48), back(z, 72), block_time - back(z, 96))
    for q in range(6):
        held = x if q < 3 else v
        for s in range(CAP):
            at = CAP * (q % 3) + s
            splat[pl.ds((q * CAP + s) * NROW, NROW), :] = jnp.broadcast_to(
                held[:, at : at + 1], (NROW, LANES)
            )


def add_pairs(sums, sources, target):
    dx, dy, dz, du, dv, dw = (sources[q] - target[q] for q in range(6))
    radius_sq = (dx * dx + dy * dy + dz * dz) + softening
    inverse = lax.rsqrt(radius_sq)
    inverse_sq = inverse * inverse
    weight = sources[6] * inverse * inverse_sq
    closing = (dx * du + dy * dv + dz * dw) * inverse_sq
    fx, fy, fz = weight * dx, weight * dy, weight * dz
    return (
        sums[0] + fx,
        sums[1] + fy,
        sums[2] + fz,
        sums[3] + weight * du,
        sums[4] + weight * dv,
        sums[5] + weight * dw,
        sums[6] + closing * fx,
        sums[7] + closing * fy,
        sums[8] + closing * fz,
    )


def force_and_jerk(sums):
    return [*sums[:3], *(sums[n] - 3.0 * sums[n + 3] for n in range(3, 6))]


def wide_row(ref, q, r):
    return jnp.broadcast_to(ref[q, pl.ds(r, 1), :], (8, LANES))


def sum_listed(source, splat, part, plan):
    count = plan.make()
    chunks = source.shape[1] // 8
    part[...] = jnp.zeros(part.shape, jnp.float32)
    zero = jnp.zeros((8, LANES), jnp.float32)

    def some_targets(n, carry):
        for u in range(AT_ONCE):
            i = plan.lists[AT_ONCE * n + u]
            target = [
                jnp.broadcast_to(splat[pl.ds(q * TARGETS + i, 1), :], (8, LANES)) for q in range(6)
            ]
            sums = (zero,) * 9
            for c in range(chunks):
                sums = add_pairs(sums, [source[q, pl.ds(8 * c, 8), :] for q in range(7)], target)
            sums = force_and_jerk(sums)
            for q in range(6):
                part[pl.ds(q * TARGETS + i, 1), :] = jnp.sum(sums[q], axis=0, keepdims=True)
        return carry

    lax.fori_loop(0, (count + AT_ONCE - 1) // AT_ONCE, some_targets, 0)


def pack_sums(part):
    lane = lane_of((8, LANES))
    total = jnp.zeros((8, LANES), jnp.float32)
    for q in range(6):
        for g in range(GROUPS):
            line = jnp.sum(part[pl.ds(q * TARGETS + 8 * g, 8), :], axis=1, keepdims=True)
            total = jnp.where(lane == 64 * (g % 2) + CAP * q + g // 2, line, total)
    return total


def load_masses(raw, ncol):
    return [raw[pl.ds(16 * h + 15, ncol, stride=32), :] for h in range(2)]


def first_force_kernel(ncol, raw, target_rows, sums_out, *work):
    *plan_work, source, splat, part = work
    plan = Plan(target_rows, 0, *plan_work)
    predict_sources(raw, source, step_size, ncol)
    for h, mass in enumerate(load_masses(raw, ncol)):
        source[6, pl.ds(h * ncol, ncol), :] = mass
    spread_targets(target_rows_at(target_rows, 0), splat, step_size)
    sum_listed(source, splat, part, plan)
    sums_out[...] = jnp.broadcast_to(pack_sums(part)[None], sums_out.shape)


def target_rows_at(target_rows, n):
    return target_rows[pl.ds(n, NROW, stride=CAP), :]


def take_over(rows, names, wanted, values):
    real = wanted < float(STARS)
    for d in range(CAP):
        rows = jnp.where((turn(names, d) == wanted) & real, turn(values, d), rows)
    return rows


def static_kernel(step, ncol, *refs):
    raw, target_rows = refs[:2]
    corrected, refs = refs[2 : 2 + step], refs[2 + step :]
    total_out, splat, targets, *plan_work, source, part = refs
    block_time = (step + 1) * step_size
    plan = Plan(target_rows, step, *plan_work)
    rows = target_rows_at(target_rows, step)
    wanted = target_rows_at(target_rows, STEPS + step)
    for j in range(step):
        names = target_rows_at(target_rows, STEPS + j)
        rows = take_over(rows, names, wanted, corrected[j][...])
    targets[...] = rows
    spread_targets(rows, splat, block_time)
    predict_sources(raw, source, block_time, ncol)
    masses = load_masses(raw, ncol)
    names = raw[pl.ds(13, ncol, stride=32), :]
    lane = lane_of((ncol, LANES)).astype(jnp.float32)
    for at in range(CAP * step):
        named = jnp.broadcast_to(names[:, at : at + 1], (ncol, LANES))
        for h in range(2):
            masses[h] = jnp.where(named == lane + float(h * LANES), 0.0, masses[h])
    for h in range(2):
        source[6, pl.ds(h * ncol, ncol), :] = masses[h]
    sum_listed(source, splat, part, plan)
    total_out[...] = pack_sums(part)


def to_columns(x):
    group = lane_of((16, LANES)) // CAP
    row = row_of((16, LANES))
    out = x
    for d in range(16):
        moved = pltpu.roll(x, CAP * d, 1) if d else x
        moved = pltpu.roll(moved, 16 - d, 0) if d else moved
        out = moved if d == 0 else jnp.where(group == (row + d) % 16, moved, out)
    return out


def fresh_kernel(step, ncol, *refs):
    total_in, splat, fresh, *refs = refs
    if step > 1:
        older, *refs = refs
    sums_out, columns, source = refs
    halves = max(ncol // 16, 1)
    blocks = halves * step
    first = halves * (step - 1)
    for h in range(halves):
        columns[pl.ds(16 * (first + h), 16), :] = to_columns(fresh[pl.ds(16 * h, 16), :])
    if step > 1:
        columns[pl.ds(0, 16 * first), :] = older[...]
        for h in range(halves):
            later = columns[pl.ds(16 * (first + h) + 13, 1), :]
            for j in range(step - 1):
                at = 16 * (halves * j + h)
                names = columns[pl.ds(at + 13, 1), :]
                again = jnp.zeros((1, LANES), jnp.float32)
                for d in range(CAP):
                    again = jnp.where(turn(later, d) == names, 1.0, again)
                mass = columns[pl.ds(at + 15, 1), :]
                columns[pl.ds(at + 15, 1), :] = jnp.where(again > 0.5, 0.0, mass)
    for b in range(blocks):
        tau = (step - b // halves) * step_size

        def load(q):
            return columns[pl.ds(16 * b + q, 1), :]

        for c in range(3):
            x, v = predict(load(c), load(3 + c), load(6 + c), load(9 + c), tau)
            source[c, b : b + 1, :] = x
            source[3 + c, b : b + 1, :] = v
        source[6, b : b + 1, :] = load(15)
    lane = lane_of((8, LANES))
    total = total_in[...]
    zero = jnp.zeros((8, LANES), jnp.float32)
    for g in range(GROUPS):
        target = [splat[pl.ds(q * TARGETS + 8 * g, 8), :] for q in range(6)]
        sums = (zero,) * 9
        for b in range(blocks):
            sums = add_pairs(sums, [wide_row(source, q, b) for q in range(7)], target)
        sums = force_and_jerk(sums)
        for q in range(6):
            line = jnp.sum(sums[q], axis=1, keepdims=True)
            total = jnp.where(lane == 64 * (g % 2) + CAP * q + g // 2, total + line, total)
    if step == STEPS - 1:
        upper = back(total, 64)
        for r in range(CAP):
            sums_out[r] = total[r : r + 1]
            sums_out[CAP + r] = upper[r : r + 1]
    else:
        sums_out[...] = jnp.broadcast_to(total[None], sums_out.shape)


def correct(old_acc, old_jerk, new_acc, new_jerk, interval):
    diff = old_acc - new_acc
    interval_sq = interval * interval
    second = (-6.0 * diff - interval * (4.0 * old_jerk + 2.0 * new_jerk)) / interval_sq
    third = (12.0 * diff + 6.0 * interval * (old_jerk + new_jerk)) / (interval_sq * interval)
    pos_step = interval_sq * interval_sq * (second / 24.0 + interval * third / 120.0)
    vel_step = interval_sq * interval * (second / 6.0 + interval * third / 24.0)
    return (pos_step, vel_step)


def add_peers(gathered):
    total = gathered[0]
    for p in range(1, NROW):
        total = total + gathered[p]
    return jnp.concatenate([total, back(total, 64)], axis=0)


def correct_rows(step, total, z, names):
    block_time = (step + 1) * step_size
    lane = lane_of(z.shape)
    tau = block_time - back(z, 96)
    old_acc, old_jerk = back(z, 48), back(z, 72)
    x, v = predict(z, back(z, 24), old_acc, old_jerk, tau)
    new_a, new_j = total, back(total, 24)
    pos_step, vel_step = correct(old_acc, old_jerk, new_a, new_j, tau)

    def lay(*parts):
        out = parts[-1]
        for n in reversed(range(len(parts) - 1)):
            piece = pltpu.roll(parts[n], 24 * n, 1) if n else parts[n]
            out = jnp.where(lane < 24 * (n + 1), piece, out)
        return out

    filled = names < float(STARS)
    rest = jnp.where(lane < 120, block_time, z)
    corrected = lay(x + pos_step, v + vel_step, new_a, new_j, rest)
    terms = lay(new_a, new_j, pos_step, vel_step, jnp.zeros_like(z))
    return jnp.where(filled, corrected, 0.0), jnp.where(filled, terms, 0.0)


def correct_kernel(step, me_of, *refs):
    gathered, target_rows, *refs = refs
    targets = None
    if step > 0:
        targets, *refs = refs
    corrected_out, fresh_out, terms_out, keep = refs
    me = me_of()
    z = target_rows_at(target_rows, 0) if step == 0 else targets[...]
    names = target_rows_at(target_rows, STEPS + step)
    corrected, terms = correct_rows(step, add_peers(gathered), z, names)
    lane = lane_of((NROW, LANES))
    keep[0] = terms
    terms_out[...] = keep[0, pl.ds(me, 1), :]
    keep[1] = jnp.where((lane >= 104) & (lane < 112), names, corrected)
    fresh_out[...] = jnp.broadcast_to(keep[1, pl.ds(me, 1), :][None], fresh_out.shape)
    corrected_out[...] = corrected


def spread(line):
    diagonal = lane_of((16, LANES)) // CAP == row_of((16, LANES))
    x = jnp.where(diagonal, jnp.broadcast_to(line, (16, LANES)), 0.0)
    for shift in (64, 32, 16, 8):
        x = x + pltpu.roll(x, shift, 1)
    return x


def put(whole, names, line):
    columns = spread(line)
    star = lane_of((16, STARS)).astype(jnp.float32)
    for s in range(CAP):
        whole = jnp.where(star == names[:, s : s + 1], columns[:, s : s + 1], whole)
    return whole


def slot_terms(line):
    return jnp.transpose(spread(line))[0:CAP, 0:12]


def last_kernel(me_of, *refs):
    gathered, target_rows, targets, state = refs[:4]
    corrected, terms = refs[4 : STEPS + 3], refs[STEPS + 3 : 2 * STEPS + 2]
    new_pos, new_vel, new_acc, new_jerk, terms_out = refs[2 * STEPS + 2 :]
    me = me_of()
    names = [target_rows[pl.ds(CAP * me + STEPS + j, 1), :] for j in range(STEPS)]
    total = jnp.sum(gathered[...], axis=0, keepdims=True)
    own, own_terms = correct_rows(STEPS - 1, total, targets[pl.ds(me, 1), :], names[-1])
    whole = state[...]
    for j in range(STEPS):
        last = j == STEPS - 1
        whole = put(whole, names[j], own if last else corrected[j][pl.ds(me, 1), :])
        terms_out[j] = slot_terms(own_terms if last else terms[j][...])
    for n, out in enumerate((new_pos, new_vel, new_acc, new_jerk)):
        out[...] = whole[3 * n : 3 * n + 3, :]


def struct(*shape):
    return jax.ShapeDtypeStruct(shape, jnp.float32)


def scratch(*shape):
    return pltpu.VMEM(shape, jnp.float32)


vmem = pl.BlockSpec(memory_space=pltpu.VMEM)
hbm = pl.BlockSpec(memory_space=pltpu.HBM)
smem = pl.BlockSpec(memory_space=pltpu.SMEM)
anywhere = pl.BlockSpec(memory_space=pl.ANY)


def call(kernel, operands, outs, work, specs=None, out_specs=None, flops=None):
    cost = None
    if flops:
        cost = pl.CostEstimate(flops=flops, bytes_accessed=1 << 20, transcendentals=0)
    return pl.pallas_call(
        kernel,
        out_shape=tuple(outs),
        in_specs=specs or [vmem] * len(operands),
        out_specs=out_specs or (vmem,) * len(outs),
        scratch_shapes=work,
        cost_estimate=cost,
        compiler_params=pltpu.CompilerParams(vmem_limit_bytes=8 << 20),
    )(*operands)


def send_all(x, axes):
    return lax.all_to_all(x, axes, split_axis=0, concat_axis=0, tiled=True)


def body(sizes, row_axes, col_axes, pos, vel, acc, jerk, masses, levels, active):
    masses, levels = masses.reshape(1, STARS), levels.reshape(1, STARS)
    pos, vel, acc, jerk, masses, levels, active = (
        pltpu.with_memory_space_constraint(a, pltpu.HBM)
        for a in (pos, vel, acc, jerk, masses, levels, active)
    )
    ncol = math.prod(sizes[axis] for axis in col_axes)

    def me_of():
        me = 0
        for axis in row_axes:
            me = me * sizes[axis] + lax.axis_index(axis)
        return me

    block, rows, state = call(
        pack_kernel,
        (pos, vel, acc, jerk, masses, levels, active),
        (struct(ncol, 32, LANES), struct(NROW, 8, LANES), struct(16, STARS)),
        [scratch(3, STARS)] * 4
        + [scratch(1, STARS), pltpu.VMEM((1, STARS), jnp.int32)]
        + [pltpu.SMEM((STEPS, CAP), jnp.int32)]
        + [scratch(32, LANES), scratch(8, LANES), pltpu.SemaphoreType.DMA((7,))],
        [hbm] * 7,
    )
    target_rows = send_all(rows, row_axes).reshape(NROW * 8, LANES)
    block, target_rows = lax.optimization_barrier((block, target_rows))
    raw = send_all(block, col_axes).reshape(ncol * 32, LANES)

    sums_shape = struct(NROW, NROW // 2, LANES)
    source_shape = (7, 2 * ncol, LANES)
    slots = struct(NROW, LANES)
    splat_shape = (6 * TARGETS, LANES)
    plan_work = [
        pltpu.VMEM((8, LANES), jnp.int32),
        pltpu.SMEM((8, LANES), jnp.int32),
        pltpu.SemaphoreType.DMA,
        pltpu.SMEM((LIST,), jnp.int32),
    ]
    source_work, splat_work = scratch(*source_shape), scratch(*splat_shape)
    (sums,) = call(
        functools.partial(first_force_kernel, ncol),
        (raw, target_rows),
        (sums_shape,),
        [*plan_work, source_work, splat_work, splat_work],
    )
    corrected, terms = [], []
    targets = columns = None
    for step in range(STEPS):
        gathered = send_all(sums, row_axes)
        if step == STEPS - 1:
            break
        operands = [gathered, target_rows] + ([] if step == 0 else [targets])
        done, fresh, own_terms = call(
            functools.partial(correct_kernel, step, me_of),
            operands,
            (slots, struct(ncol, 1, LANES), struct(1, LANES)),
            [scratch(2, NROW, LANES)],
        )
        corrected.append(done)
        terms.append(own_terms)
        fresh = send_all(fresh, col_axes).reshape(ncol, LANES)
        static, splat, targets = call(
            functools.partial(static_kernel, step + 1, ncol),
            (raw, target_rows, *corrected),
            (struct(8, LANES), struct(*splat_shape), slots),
            [*plan_work, source_work, splat_work],
            flops=3 * 10**7,
        )
        blocks = max(ncol // 16, 1) * (step + 1)
        operands = [static, splat, fresh] + ([] if step == 0 else [columns])
        outs, work = [sums_shape], [scratch(7, blocks, LANES)]
        if step + 1 < STEPS - 1:
            outs.append(struct(16 * blocks, LANES))
        else:
            outs[0] = struct(NROW, 1, LANES)
            work.insert(0, scratch(16 * blocks, LANES))
        sums, *columns = call(
            functools.partial(fresh_kernel, step + 1, ncol), operands, outs, work
        )
        if columns:
            (columns,) = columns
    *new, slot_rows = call(
        functools.partial(last_kernel, me_of),
        (gathered.reshape(NROW, LANES), target_rows, targets, state, *corrected, *terms),
        (struct(3, STARS),) * 4 + (struct(STEPS, CAP, 12),),
        [],
    )
    return (*new, jnp.swapaxes(slot_rows, 1, 2))


def solution(mesh):
    sizes = {"x": 4, "z": mesh.shape["wide"] // 8, "core": 2, "narrow": mesh.shape["narrow"]}
    row_axes, col_axes = ("core", "narrow"), ("z", "x")
    every = tuple(sizes)
    finer = Mesh(mesh.devices.reshape(tuple(sizes.values())), every)
    in_specs = (P(None, every),) * 4 + (P(every), P(every), P(None, every))
    out_specs = (P(None, every),) * 4 + (P(None, None, every),)
    return jax.shard_map(
        functools.partial(body, sizes, row_axes, col_axes),
        mesh=finer,
        in_specs=in_specs,
        out_specs=out_specs,
        check_vma=False,
    )
```

```python
import functools
import math

import jax
import jax.numpy as jnp
from jax import lax
from jax.experimental import pallas as pl
from jax.experimental.pallas import tpu as pltpu
from jax.sharding import Mesh, PartitionSpec as P

step_size = 1.0 / 32.0
softening = 2.5e-05
STEPS = 4
CAP = 8
LANES = 128
STARS = 256

NROW = 16
TARGETS = NROW * CAP
GROUPS = TARGETS // 8
BLOCK = 29
AT_ONCE = 8
LIST = TARGETS + 32


def predict(x, v, a, j, tau):
    ahead_x = x + tau * (v + tau * (a * 0.5 + tau * j / 6.0))
    ahead_v = v + tau * (a + tau * j * 0.5)
    return ahead_x, ahead_v


def back(x, lanes):
    return pltpu.roll(x, LANES - lanes, 1) if lanes else x


def lane_of(shape):
    return lax.broadcasted_iota(jnp.int32, shape, 1)


def row_of(shape):
    return lax.broadcasted_iota(jnp.int32, shape, 0)


def turn(x, d):
    if d == 0:
        return x
    slot = lane_of(x.shape) % CAP
    return jnp.where(slot < CAP - d, pltpu.roll(x, LANES - d, 1), pltpu.roll(x, CAP - d, 1))


def fetch(sources, held, sems):
    copies = [pltpu.make_async_copy(a, b, sems.at[n]) for n, (a, b) in enumerate(zip(sources, held))]
    for copy in copies:
        copy.start()
    return copies


def pack_kernel(*refs):
    block_out, row_out, state, *held = refs[7:17]
    block, rows, sems = refs[17:]
    for copy in fetch(refs[:7], held, sems):
        copy.wait()
    pos, vel, acc, jerk, mass, levels, active = held
    for n, part in enumerate((pos, vel, acc, jerk)):
        state[3 * n : 3 * n + 3, :] = part[...]
    times = step_size * (1.0 - jnp.left_shift(1, levels[...]).astype(jnp.float32))
    state[12:15, :] = jnp.broadcast_to(times, (3, STARS))
    state[15:16, :] = mass[...]
    whole = state[...]
    lane = lane_of((1, LANES))
    names = jnp.full((1, LANES), STARS, jnp.int32)
    for k in range(STEPS):
        for s in range(CAP):
            names = jnp.where(lane == CAP * k + s, active[k, s], names)
    for h in range(2):
        block[14 * h : 14 * h + 13, :] = whole[0:13, LANES * h : LANES * h + LANES]
        block[14 * h + 13 : 14 * h + 14, :] = whole[15:16, LANES * h : LANES * h + LANES]
    block[28:29, :] = names.astype(jnp.float32)
    filled = block[0:BLOCK, :]
    for p in range(block_out.shape[0] // BLOCK):
        block_out[BLOCK * p : BLOCK * p + BLOCK, :] = filled
    lane = lane_of((16, LANES))
    diagonal = lane // CAP == row_of((16, LANES))
    slot = lane % CAP
    star = lane_of((1, STARS))
    for k in range(STEPS):
        table = jnp.zeros((16, LANES), jnp.float32)
        names = jnp.zeros((1, LANES), jnp.float32)
        for s in range(CAP):
            named = active[k, s]
            column = jnp.sum(jnp.where(star == named, whole, 0.0), axis=1, keepdims=True)
            table = jnp.where(slot == s, column, table)
            names = jnp.where(slot[0:1] == s, named.astype(jnp.float32), names)
        rows[k : k + 1, :] = jnp.sum(jnp.where(diagonal, table, 0.0), axis=0, keepdims=True)
        rows[STEPS + k : STEPS + k + 1, :] = names
    row_out[...] = jnp.broadcast_to(rows[...][None], row_out.shape)


class Plan:
    def __init__(self, target_rows, step, counts, scalars, sem, lists):
        self.scalars, self.lists = scalars, lists
        names = target_rows_at(target_rows, STEPS + step)
        lane = lane_of((NROW, LANES))
        named = jnp.where((names < float(STARS)) & (lane < CAP), 1.0, 0.0)
        count = jnp.sum(named, axis=1, keepdims=True)
        count = jnp.where(lane == row_of((NROW, LANES)), count, 0.0)
        count = jnp.sum(count, axis=0, keepdims=True).astype(jnp.int32)
        counts[...] = jnp.broadcast_to(count, (8, LANES))
        self.copy = pltpu.make_async_copy(counts, scalars, sem)
        self.copy.start()

    def make(self):
        self.copy.wait()
        n = 0
        for r in range(NROW):
            for s in range(CAP):
                self.lists[n + s] = NROW * s + r
            n = n + self.scalars[0, r]
        for u in range(AT_ONCE):
            self.lists[n + u] = 0
        return n


def predict_sources(raw, source, block_time, ncol):
    for h in range(2):
        at = pl.ds(h * ncol, ncol)

        def load(q):
            return raw[pl.ds(14 * h + q, ncol, stride=BLOCK), :]

        tau = block_time - load(12)
        for c in range(3):
            x, v = predict(load(c), load(3 + c), load(6 + c), load(9 + c), tau)
            source[c, at, :] = x
            source[3 + c, at, :] = v


def spread_targets(z, splat, block_time):
    x, v = predict(z, back(z, 24), back(z, 48), back(z, 72), block_time - back(z, 96))
    for q in range(6):
        held = x if q < 3 else v
        for s in range(CAP):
            at = CAP * (q % 3) + s
            splat[pl.ds((q * CAP + s) * NROW, NROW), :] = jnp.broadcast_to(
                held[:, at : at + 1], (NROW, LANES)
            )


def add_pairs(sums, sources, target):
    dx, dy, dz, du, dv, dw = (sources[q] - target[q] for q in range(6))
    radius_sq = (dx * dx + dy * dy + dz * dz) + softening
    inverse = lax.rsqrt(radius_sq)
    inverse_sq = inverse * inverse
    weight = sources[6] * inverse * inverse_sq
    closing = (dx * du + dy * dv + dz * dw) * inverse_sq
    fx, fy, fz = weight * dx, weight * dy, weight * dz
    return (
        sums[0] + fx,
        sums[1] + fy,
        sums[2] + fz,
        sums[3] + weight * du,
        sums[4] + weight * dv,
        sums[5] + weight * dw,
        sums[6] + closing * fx,
        sums[7] + closing * fy,
        sums[8] + closing * fz,
    )


def force_and_jerk(sums):
    return [*sums[:3], *(sums[n] - 3.0 * sums[n + 3] for n in range(3, 6))]


def wide_row(ref, q, r):
    return jnp.broadcast_to(ref[q, pl.ds(r, 1), :], (8, LANES))


def sum_listed(source, splat, part, plan):
    count = plan.make()
    chunks = source.shape[1] // 8
    part[...] = jnp.zeros(part.shape, jnp.float32)
    zero = jnp.zeros((8, LANES), jnp.float32)

    def some_targets(n, carry):
        for u in range(AT_ONCE):
            i = plan.lists[AT_ONCE * n + u]
            target = [
                jnp.broadcast_to(splat[pl.ds(q * TARGETS + i, 1), :], (8, LANES)) for q in range(6)
            ]
            sums = (zero,) * 9
            for c in range(chunks):
                sums = add_pairs(sums, [source[q, pl.ds(8 * c, 8), :] for q in range(7)], target)
            sums = force_and_jerk(sums)
            for q in range(6):
                part[pl.ds(q * TARGETS + i, 1), :] = jnp.sum(sums[q], axis=0, keepdims=True)
        return carry

    lax.fori_loop(0, (count + AT_ONCE - 1) // AT_ONCE, some_targets, 0)


def pack_sums(part):
    lane = lane_of((8, LANES))
    total = jnp.zeros((8, LANES), jnp.float32)
    for q in range(6):
        for g in range(GROUPS):
            line = jnp.sum(part[pl.ds(q * TARGETS + 8 * g, 8), :], axis=1, keepdims=True)
            total = jnp.where(lane == 64 * (g % 2) + CAP * q + g // 2, line, total)
    return total


def load_masses(raw, ncol):
    return [raw[pl.ds(14 * h + 13, ncol, stride=BLOCK), :] for h in range(2)]


def first_force_kernel(ncol, raw, target_rows, sums_out, *work):
    *plan_work, source, splat, part = work
    plan = Plan(target_rows, 0, *plan_work)
    predict_sources(raw, source, step_size, ncol)
    for h, mass in enumerate(load_masses(raw, ncol)):
        source[6, pl.ds(h * ncol, ncol), :] = mass
    spread_targets(target_rows_at(target_rows, 0), splat, step_size)
    sum_listed(source, splat, part, plan)
    sums_out[...] = jnp.broadcast_to(pack_sums(part)[None], sums_out.shape)


def target_rows_at(target_rows, n):
    return target_rows[pl.ds(n, NROW, stride=CAP), :]


def take_over(rows, names, wanted, values):
    real = wanted < float(STARS)
    for d in range(CAP):
        rows = jnp.where((turn(names, d) == wanted) & real, turn(values, d), rows)
    return rows


def static_kernel(step, ncol, *refs):
    raw, target_rows = refs[:2]
    corrected, refs = refs[2 : 2 + step], refs[2 + step :]
    total_out, splat, targets, *plan_work, source, part = refs
    block_time = (step + 1) * step_size
    plan = Plan(target_rows, step, *plan_work)
    rows = target_rows_at(target_rows, step)
    wanted = target_rows_at(target_rows, STEPS + step)
    for j in range(step):
        names = target_rows_at(target_rows, STEPS + j)
        rows = take_over(rows, names, wanted, corrected[j][...])
    targets[...] = rows
    spread_targets(rows, splat, block_time)
    predict_sources(raw, source, block_time, ncol)
    masses = load_masses(raw, ncol)
    names = raw[pl.ds(28, ncol, stride=BLOCK), :]
    lane = lane_of((ncol, LANES)).astype(jnp.float32)
    for at in range(CAP * step):
        named = jnp.broadcast_to(names[:, at : at + 1], (ncol, LANES))
        for h in range(2):
            masses[h] = jnp.where(named == lane + float(h * LANES), 0.0, masses[h])
    for h in range(2):
        source[6, pl.ds(h * ncol, ncol), :] = masses[h]
    sum_listed(source, splat, part, plan)
    total_out[...] = pack_sums(part)


def to_columns(x):
    group = lane_of((16, LANES)) // CAP
    row = row_of((16, LANES))
    out = x
    for d in range(16):
        moved = pltpu.roll(x, CAP * d, 1) if d else x
        moved = pltpu.roll(moved, 16 - d, 0) if d else moved
        out = moved if d == 0 else jnp.where(group == (row + d) % 16, moved, out)
    return out


def fresh_kernel(step, ncol, *refs):
    total_in, splat, fresh, *refs = refs
    if step > 1:
        older, *refs = refs
    sums_out, columns, source = refs
    halves = max(ncol // 16, 1)
    blocks = halves * step
    first = halves * (step - 1)
    for h in range(halves):
        columns[pl.ds(16 * (first + h), 16), :] = to_columns(fresh[pl.ds(16 * h, 16), :])
    if step > 1:
        columns[pl.ds(0, 16 * first), :] = older[...]
        for h in range(halves):
            later = columns[pl.ds(16 * (first + h) + 13, 1), :]
            for j in range(step - 1):
                at = 16 * (halves * j + h)
                names = columns[pl.ds(at + 13, 1), :]
                again = jnp.zeros((1, LANES), jnp.float32)
                for d in range(CAP):
                    again = jnp.where(turn(later, d) == names, 1.0, again)
                mass = columns[pl.ds(at + 15, 1), :]
                columns[pl.ds(at + 15, 1), :] = jnp.where(again > 0.5, 0.0, mass)
    for b in range(blocks):
        tau = (step - b // halves) * step_size

        def load(q):
            return columns[pl.ds(16 * b + q, 1), :]

        for c in range(3):
            x, v = predict(load(c), load(3 + c), load(6 + c), load(9 + c), tau)
            source[c, b : b + 1, :] = x
            source[3 + c, b : b + 1, :] = v
        source[6, b : b + 1, :] = load(15)
    lane = lane_of((8, LANES))
    total = total_in[...]
    zero = jnp.zeros((8, LANES), jnp.float32)
    for g in range(GROUPS):
        target = [splat[pl.ds(q * TARGETS + 8 * g, 8), :] for q in range(6)]
        sums = (zero,) * 9
        for b in range(blocks):
            sums = add_pairs(sums, [wide_row(source, q, b) for q in range(7)], target)
        sums = force_and_jerk(sums)
        for q in range(6):
            line = jnp.sum(sums[q], axis=1, keepdims=True)
            total = jnp.where(lane == 64 * (g % 2) + CAP * q + g // 2, total + line, total)
    if step == STEPS - 1:
        upper = back(total, 64)
        for r in range(CAP):
            sums_out[r] = total[r : r + 1]
            sums_out[CAP + r] = upper[r : r + 1]
    else:
        sums_out[...] = jnp.broadcast_to(total[None], sums_out.shape)


def correct(old_acc, old_jerk, new_acc, new_jerk, interval):
    diff = old_acc - new_acc
    interval_sq = interval * interval
    second = (-6.0 * diff - interval * (4.0 * old_jerk + 2.0 * new_jerk)) / interval_sq
    third = (12.0 * diff + 6.0 * interval * (old_jerk + new_jerk)) / (interval_sq * interval)
    pos_step = interval_sq * interval_sq * (second / 24.0 + interval * third / 120.0)
    vel_step = interval_sq * interval * (second / 6.0 + interval * third / 24.0)
    return (pos_step, vel_step)


def add_peers(gathered):
    total = gathered[0]
    for p in range(1, NROW):
        total = total + gathered[p]
    return jnp.concatenate([total, back(total, 64)], axis=0)


def correct_rows(step, total, z, names):
    block_time = (step + 1) * step_size
    lane = lane_of(z.shape)
    tau = block_time - back(z, 96)
    old_acc, old_jerk = back(z, 48), back(z, 72)
    x, v = predict(z, back(z, 24), old_acc, old_jerk, tau)
    new_a, new_j = total, back(total, 24)
    pos_step, vel_step = correct(old_acc, old_jerk, new_a, new_j, tau)

    def lay(*parts):
        out = parts[-1]
        for n in reversed(range(len(parts) - 1)):
            piece = pltpu.roll(parts[n], 24 * n, 1) if n else parts[n]
            out = jnp.where(lane < 24 * (n + 1), piece, out)
        return out

    filled = names < float(STARS)
    rest = jnp.where(lane < 120, block_time, z)
    corrected = lay(x + pos_step, v + vel_step, new_a, new_j, rest)
    terms = lay(new_a, new_j, pos_step, vel_step, jnp.zeros_like(z))
    return jnp.where(filled, corrected, 0.0), jnp.where(filled, terms, 0.0)


def correct_kernel(step, me_of, *refs):
    gathered, target_rows, *refs = refs
    targets = None
    if step > 0:
        targets, *refs = refs
    corrected_out, fresh_out, terms_out, keep = refs
    me = me_of()
    z = target_rows_at(target_rows, 0) if step == 0 else targets[...]
    names = target_rows_at(target_rows, STEPS + step)
    corrected, terms = correct_rows(step, add_peers(gathered), z, names)
    lane = lane_of((NROW, LANES))
    keep[0] = terms
    terms_out[...] = keep[0, pl.ds(me, 1), :]
    keep[1] = jnp.where((lane >= 104) & (lane < 112), names, corrected)
    fresh_out[...] = jnp.broadcast_to(keep[1, pl.ds(me, 1), :][None], fresh_out.shape)
    corrected_out[...] = corrected


def spread(line):
    diagonal = lane_of((16, LANES)) // CAP == row_of((16, LANES))
    x = jnp.where(diagonal, jnp.broadcast_to(line, (16, LANES)), 0.0)
    for shift in (64, 32, 16, 8):
        x = x + pltpu.roll(x, shift, 1)
    return x


def put(whole, names, line):
    columns = spread(line)
    star = lane_of((16, STARS)).astype(jnp.float32)
    for s in range(CAP):
        whole = jnp.where(star == names[:, s : s + 1], columns[:, s : s + 1], whole)
    return whole


def slot_terms(line):
    return jnp.transpose(spread(line))[0:CAP, 0:12]


def last_kernel(me_of, *refs):
    gathered, target_rows, targets, state = refs[:4]
    corrected, terms = refs[4 : STEPS + 3], refs[STEPS + 3 : 2 * STEPS + 2]
    new_pos, new_vel, new_acc, new_jerk, terms_out = refs[2 * STEPS + 2 :]
    me = me_of()
    names = [target_rows[pl.ds(CAP * me + STEPS + j, 1), :] for j in range(STEPS)]
    total = jnp.sum(gathered[...], axis=0, keepdims=True)
    own, own_terms = correct_rows(STEPS - 1, total, targets[pl.ds(me, 1), :], names[-1])
    whole = state[...]
    for j in range(STEPS):
        last = j == STEPS - 1
        whole = put(whole, names[j], own if last else corrected[j][pl.ds(me, 1), :])
        terms_out[j] = slot_terms(own_terms if last else terms[j][...])
    for n, out in enumerate((new_pos, new_vel, new_acc, new_jerk)):
        out[...] = whole[3 * n : 3 * n + 3, :]


def struct(*shape):
    return jax.ShapeDtypeStruct(shape, jnp.float32)


def scratch(*shape):
    return pltpu.VMEM(shape, jnp.float32)


vmem = pl.BlockSpec(memory_space=pltpu.VMEM)
hbm = pl.BlockSpec(memory_space=pltpu.HBM)
smem = pl.BlockSpec(memory_space=pltpu.SMEM)
anywhere = pl.BlockSpec(memory_space=pl.ANY)


def call(kernel, operands, outs, work, specs=None, out_specs=None, flops=None):
    cost = None
    if flops:
        cost = pl.CostEstimate(flops=flops, bytes_accessed=1 << 20, transcendentals=0)
    return pl.pallas_call(
        kernel,
        out_shape=tuple(outs),
        in_specs=specs or [vmem] * len(operands),
        out_specs=out_specs or (vmem,) * len(outs),
        scratch_shapes=work,
        cost_estimate=cost,
        compiler_params=pltpu.CompilerParams(vmem_limit_bytes=8 << 20),
    )(*operands)


def send_all(x, axes):
    return lax.all_to_all(x, axes, split_axis=0, concat_axis=0, tiled=True)


def body(sizes, row_axes, col_axes, pos, vel, acc, jerk, masses, levels, active):
    masses, levels = masses.reshape(1, STARS), levels.reshape(1, STARS)
    pos, vel, acc, jerk, masses, levels, active = (
        pltpu.with_memory_space_constraint(a, pltpu.HBM)
        for a in (pos, vel, acc, jerk, masses, levels, active)
    )
    ncol = math.prod(sizes[axis] for axis in col_axes)

    def me_of():
        me = 0
        for axis in row_axes:
            me = me * sizes[axis] + lax.axis_index(axis)
        return me

    block, rows, state = call(
        pack_kernel,
        (pos, vel, acc, jerk, masses, levels, active),
        (struct(ncol * BLOCK, LANES), struct(NROW, 8, LANES), struct(16, STARS)),
        [scratch(3, STARS)] * 4
        + [scratch(1, STARS), pltpu.VMEM((1, STARS), jnp.int32)]
        + [pltpu.SMEM((STEPS, CAP), jnp.int32)]
        + [scratch(32, LANES), scratch(8, LANES), pltpu.SemaphoreType.DMA((7,))],
        [hbm] * 7,
    )
    target_rows = send_all(rows, row_axes).reshape(NROW * 8, LANES)
    block, target_rows = lax.optimization_barrier((block, target_rows))
    block = block.reshape(ncol, 1, BLOCK * LANES)
    raw = send_all(block, col_axes).reshape(ncol * BLOCK, LANES)

    sums_shape = struct(NROW, NROW // 2, LANES)
    source_shape = (7, 2 * ncol, LANES)
    slots = struct(NROW, LANES)
    splat_shape = (6 * TARGETS, LANES)
    plan_work = [
        pltpu.VMEM((8, LANES), jnp.int32),
        pltpu.SMEM((8, LANES), jnp.int32),
        pltpu.SemaphoreType.DMA,
        pltpu.SMEM((LIST,), jnp.int32),
    ]
    source_work, splat_work = scratch(*source_shape), scratch(*splat_shape)
    (sums,) = call(
        functools.partial(first_force_kernel, ncol),
        (raw, target_rows),
        (sums_shape,),
        [*plan_work, source_work, splat_work, splat_work],
    )
    corrected, terms = [], []
    targets = columns = None
    for step in range(STEPS):
        gathered = send_all(sums, row_axes)
        if step == STEPS - 1:
            break
        operands = [gathered, target_rows] + ([] if step == 0 else [targets])
        done, fresh, own_terms = call(
            functools.partial(correct_kernel, step, me_of),
            operands,
            (slots, struct(ncol, 1, LANES), struct(1, LANES)),
            [scratch(2, NROW, LANES)],
        )
        corrected.append(done)
        terms.append(own_terms)
        fresh = send_all(fresh, col_axes).reshape(ncol, LANES)
        static, splat, targets = call(
            functools.partial(static_kernel, step + 1, ncol),
            (raw, target_rows, *corrected),
            (struct(8, LANES), struct(*splat_shape), slots),
            [*plan_work, source_work, splat_work],
            flops=3 * 10**7,
        )
        blocks = max(ncol // 16, 1) * (step + 1)
        operands = [static, splat, fresh] + ([] if step == 0 else [columns])
        outs, work = [sums_shape], [scratch(7, blocks, LANES)]
        if step + 1 < STEPS - 1:
            outs.append(struct(16 * blocks, LANES))
        else:
            outs[0] = struct(NROW, 1, LANES)
            work.insert(0, scratch(16 * blocks, LANES))
        sums, *columns = call(
            functools.partial(fresh_kernel, step + 1, ncol), operands, outs, work
        )
        if columns:
            (columns,) = columns
    *new, slot_rows = call(
        functools.partial(last_kernel, me_of),
        (gathered.reshape(NROW, LANES), target_rows, targets, state, *corrected, *terms),
        (struct(3, STARS),) * 4 + (struct(STEPS, CAP, 12),),
        [],
    )
    return (*new, jnp.swapaxes(slot_rows, 1, 2))


def solution(mesh):
    sizes = {"x": 4, "z": mesh.shape["wide"] // 8, "core": 2, "narrow": mesh.shape["narrow"]}
    row_axes, col_axes = ("core", "narrow"), ("z", "x")
    every = tuple(sizes)
    finer = Mesh(mesh.devices.reshape(tuple(sizes.values())), every)
    in_specs = (P(None, every),) * 4 + (P(every), P(every), P(None, every))
    out_specs = (P(None, every),) * 4 + (P(None, None, every),)
    return jax.shard_map(
        functools.partial(body, sizes, row_axes, col_axes),
        mesh=finer,
        in_specs=in_specs,
        out_specs=out_specs,
        check_vma=False,
    )
```

```python
import functools
import math

import jax
import jax.numpy as jnp
from jax import lax
from jax.experimental import pallas as pl
from jax.experimental.pallas import tpu as pltpu
from jax.sharding import Mesh, PartitionSpec as P

step_size = 1.0 / 32.0
softening = 2.5e-05
STEPS = 4
CAP = 8
LANES = 128
STARS = 256

NROW = 16
TARGETS = NROW * CAP
GROUPS = TARGETS // 8
BLOCK = 27
AT_ONCE = 8
LIST = TARGETS + 32


def predict(x, v, a, j, tau):
    ahead_x = x + tau * (v + tau * (a * 0.5 + tau * j / 6.0))
    ahead_v = v + tau * (a + tau * j * 0.5)
    return ahead_x, ahead_v


def back(x, lanes):
    return pltpu.roll(x, LANES - lanes, 1) if lanes else x


def lane_of(shape):
    return lax.broadcasted_iota(jnp.int32, shape, 1)


def row_of(shape):
    return lax.broadcasted_iota(jnp.int32, shape, 0)


def turn(x, d):
    if d == 0:
        return x
    slot = lane_of(x.shape) % CAP
    return jnp.where(slot < CAP - d, pltpu.roll(x, LANES - d, 1), pltpu.roll(x, CAP - d, 1))


def fetch(sources, held, sems):
    copies = [pltpu.make_async_copy(a, b, sems.at[n]) for n, (a, b) in enumerate(zip(sources, held))]
    for copy in copies:
        copy.start()
    return copies


def pack_kernel(*refs):
    block_out, row_out, state, *held = refs[7:17]
    moved, block, rows, sems = refs[17:]
    for copy in fetch(refs[:7], held, sems):
        copy.wait()
    pos, vel, acc, jerk, mass, levels, active = held
    for n, part in enumerate((pos, vel, acc, jerk)):
        state[3 * n : 3 * n + 3, :] = part[...]
    times = step_size * (1.0 - jnp.left_shift(1, levels[...]).astype(jnp.float32))
    state[12:16, :] = jnp.zeros((4, STARS), jnp.float32)
    tau = step_size - times
    x, v = predict(pos[...], vel[...], acc[...], jerk[...], tau)
    for n, part in enumerate((x, v, acc[...] + tau * jerk[...], jerk[...])):
        moved[3 * n : 3 * n + 3, :] = part
    moved[12:15, :] = jnp.broadcast_to(times, (3, STARS))
    moved[15:16, :] = mass[...]
    whole = moved[...]
    lane = lane_of((1, LANES))
    names = jnp.full((1, LANES), STARS, jnp.int32)
    for k in range(STEPS):
        for s in range(CAP):
            names = jnp.where(lane == CAP * k + s, active[k, s], names)
    for h in range(2):
        block[13 * h : 13 * h + 12, :] = whole[0:12, LANES * h : LANES * h + LANES]
        block[13 * h + 12 : 13 * h + 13, :] = whole[15:16, LANES * h : LANES * h + LANES]
    block[26:27, :] = names.astype(jnp.float32)
    filled = block[0:BLOCK, :]
    for p in range(block_out.shape[0] // BLOCK):
        block_out[BLOCK * p : BLOCK * p + BLOCK, :] = filled
    lane = lane_of((16, LANES))
    diagonal = lane // CAP == row_of((16, LANES))
    slot = lane % CAP
    star = lane_of((1, STARS))
    for k in range(STEPS):
        table = jnp.zeros((16, LANES), jnp.float32)
        names = jnp.zeros((1, LANES), jnp.float32)
        for s in range(CAP):
            named = active[k, s]
            column = jnp.sum(jnp.where(star == named, whole, 0.0), axis=1, keepdims=True)
            table = jnp.where(slot == s, column, table)
            names = jnp.where(slot[0:1] == s, named.astype(jnp.float32), names)
        rows[k : k + 1, :] = jnp.sum(jnp.where(diagonal, table, 0.0), axis=0, keepdims=True)
        rows[STEPS + k : STEPS + k + 1, :] = names
    row_out[...] = jnp.broadcast_to(rows[...][None], row_out.shape)


class Plan:
    def __init__(self, target_rows, step, counts, scalars, sem, lists):
        self.scalars, self.lists = scalars, lists
        names = target_rows_at(target_rows, STEPS + step)
        lane = lane_of((NROW, LANES))
        named = jnp.where((names < float(STARS)) & (lane < CAP), 1.0, 0.0)
        count = jnp.sum(named, axis=1, keepdims=True)
        count = jnp.where(lane == row_of((NROW, LANES)), count, 0.0)
        count = jnp.sum(count, axis=0, keepdims=True).astype(jnp.int32)
        counts[...] = jnp.broadcast_to(count, (8, LANES))
        self.copy = pltpu.make_async_copy(counts, scalars, sem)
        self.copy.start()

    def make(self):
        self.copy.wait()
        n = 0
        for r in range(NROW):
            for s in range(CAP):
                self.lists[n + s] = NROW * s + r
            n = n + self.scalars[0, r]
        for u in range(AT_ONCE):
            self.lists[n + u] = 0
        return n


def predict_sources(raw, source, block_time, ncol):
    for h in range(2):
        at = pl.ds(h * ncol, ncol)

        def load(q):
            return raw[pl.ds(13 * h + q, ncol, stride=BLOCK), :]

        tau = block_time - step_size
        for c in range(3):
            x, v = predict(load(c), load(3 + c), load(6 + c), load(9 + c), tau)
            source[c, at, :] = x
            source[3 + c, at, :] = v


def spread_targets(z, splat, block_time):
    tau = block_time - jnp.maximum(back(z, 96), step_size)
    x, v = predict(z, back(z, 24), back(z, 48), back(z, 72), tau)
    for q in range(6):
        held = x if q < 3 else v
        for s in range(CAP):
            at = CAP * (q % 3) + s
            splat[pl.ds((q * CAP + s) * NROW, NROW), :] = jnp.broadcast_to(
                held[:, at : at + 1], (NROW, LANES)
            )


def add_pairs(sums, sources, target):
    dx, dy, dz, du, dv, dw = (sources[q] - target[q] for q in range(6))
    radius_sq = (dx * dx + dy * dy + dz * dz) + softening
    inverse = lax.rsqrt(radius_sq)
    inverse_sq = inverse * inverse
    weight = sources[6] * inverse * inverse_sq
    closing = (dx * du + dy * dv + dz * dw) * inverse_sq
    fx, fy, fz = weight * dx, weight * dy, weight * dz
    return (
        sums[0] + fx,
        sums[1] + fy,
        sums[2] + fz,
        sums[3] + weight * du,
        sums[4] + weight * dv,
        sums[5] + weight * dw,
        sums[6] + closing * fx,
        sums[7] + closing * fy,
        sums[8] + closing * fz,
    )


def force_and_jerk(sums):
    return [*sums[:3], *(sums[n] - 3.0 * sums[n + 3] for n in range(3, 6))]


def wide_row(ref, q, r):
    return jnp.broadcast_to(ref[q, pl.ds(r, 1), :], (8, LANES))


def sum_listed(source, splat, part, plan):
    count = plan.make()
    chunks = source.shape[1] // 8
    part[...] = jnp.zeros(part.shape, jnp.float32)
    zero = jnp.zeros((8, LANES), jnp.float32)

    def some_targets(n, carry):
        for u in range(AT_ONCE):
            i = plan.lists[AT_ONCE * n + u]
            target = [
                jnp.broadcast_to(splat[pl.ds(q * TARGETS + i, 1), :], (8, LANES)) for q in range(6)
            ]
            sums = (zero,) * 9
            for c in range(chunks):
                sums = add_pairs(sums, [source[q, pl.ds(8 * c, 8), :] for q in range(7)], target)
            sums = force_and_jerk(sums)
            for q in range(6):
                part[pl.ds(q * TARGETS + i, 1), :] = jnp.sum(sums[q], axis=0, keepdims=True)
        return carry

    lax.fori_loop(0, (count + AT_ONCE - 1) // AT_ONCE, some_targets, 0)


def pack_sums(part):
    lane = lane_of((8, LANES))
    total = jnp.zeros((8, LANES), jnp.float32)
    for q in range(6):
        for g in range(GROUPS):
            line = jnp.sum(part[pl.ds(q * TARGETS + 8 * g, 8), :], axis=1, keepdims=True)
            total = jnp.where(lane == 64 * (g % 2) + CAP * q + g // 2, line, total)
    return total


def load_masses(raw, ncol):
    return [raw[pl.ds(13 * h + 12, ncol, stride=BLOCK), :] for h in range(2)]


def first_force_kernel(ncol, raw, target_rows, sums_out, *work):
    *plan_work, source, splat, part = work
    plan = Plan(target_rows, 0, *plan_work)
    predict_sources(raw, source, step_size, ncol)
    for h, mass in enumerate(load_masses(raw, ncol)):
        source[6, pl.ds(h * ncol, ncol), :] = mass
    spread_targets(target_rows_at(target_rows, 0), splat, step_size)
    sum_listed(source, splat, part, plan)
    sums_out[...] = jnp.broadcast_to(pack_sums(part)[None], sums_out.shape)


def target_rows_at(target_rows, n):
    return target_rows[pl.ds(n, NROW, stride=CAP), :]


def take_over(rows, names, wanted, values):
    real = wanted < float(STARS)
    for d in range(CAP):
        rows = jnp.where((turn(names, d) == wanted) & real, turn(values, d), rows)
    return rows


def static_kernel(step, ncol, *refs):
    raw, target_rows = refs[:2]
    corrected, refs = refs[2 : 2 + step], refs[2 + step :]
    total_out, splat, targets, *plan_work, source, part = refs
    block_time = (step + 1) * step_size
    plan = Plan(target_rows, step, *plan_work)
    rows = target_rows_at(target_rows, step)
    wanted = target_rows_at(target_rows, STEPS + step)
    for j in range(step):
        names = target_rows_at(target_rows, STEPS + j)
        rows = take_over(rows, names, wanted, corrected[j][...])
    targets[...] = rows
    spread_targets(rows, splat, block_time)
    predict_sources(raw, source, block_time, ncol)
    masses = load_masses(raw, ncol)
    names = raw[pl.ds(26, ncol, stride=BLOCK), :]
    lane = lane_of((ncol, LANES)).astype(jnp.float32)
    for at in range(CAP * step):
        named = jnp.broadcast_to(names[:, at : at + 1], (ncol, LANES))
        for h in range(2):
            masses[h] = jnp.where(named == lane + float(h * LANES), 0.0, masses[h])
    for h in range(2):
        source[6, pl.ds(h * ncol, ncol), :] = masses[h]
    sum_listed(source, splat, part, plan)
    total_out[...] = pack_sums(part)


def to_columns(x):
    group = lane_of((16, LANES)) // CAP
    row = row_of((16, LANES))
    out = x
    for d in range(16):
        moved = pltpu.roll(x, CAP * d, 1) if d else x
        moved = pltpu.roll(moved, 16 - d, 0) if d else moved
        out = moved if d == 0 else jnp.where(group == (row + d) % 16, moved, out)
    return out


def fresh_kernel(step, ncol, *refs):
    total_in, splat, fresh, *refs = refs
    if step > 1:
        older, *refs = refs
    sums_out, columns, source = refs
    halves = max(ncol // 16, 1)
    blocks = halves * step
    first = halves * (step - 1)
    for h in range(halves):
        columns[pl.ds(16 * (first + h), 16), :] = to_columns(fresh[pl.ds(16 * h, 16), :])
    if step > 1:
        columns[pl.ds(0, 16 * first), :] = older[...]
        for h in range(halves):
            later = columns[pl.ds(16 * (first + h) + 13, 1), :]
            for j in range(step - 1):
                at = 16 * (halves * j + h)
                names = columns[pl.ds(at + 13, 1), :]
                again = jnp.zeros((1, LANES), jnp.float32)
                for d in range(CAP):
                    again = jnp.where(turn(later, d) == names, 1.0, again)
                mass = columns[pl.ds(at + 15, 1), :]
                columns[pl.ds(at + 15, 1), :] = jnp.where(again > 0.5, 0.0, mass)
    for b in range(blocks):
        tau = (step - b // halves) * step_size

        def load(q):
            return columns[pl.ds(16 * b + q, 1), :]

        for c in range(3):
            x, v = predict(load(c), load(3 + c), load(6 + c), load(9 + c), tau)
            source[c, b : b + 1, :] = x
            source[3 + c, b : b + 1, :] = v
        source[6, b : b + 1, :] = load(15)
    lane = lane_of((8, LANES))
    total = total_in[...]
    zero = jnp.zeros((8, LANES), jnp.float32)
    for g in range(GROUPS):
        target = [splat[pl.ds(q * TARGETS + 8 * g, 8), :] for q in range(6)]
        sums = (zero,) * 9
        for b in range(blocks):
            sums = add_pairs(sums, [wide_row(source, q, b) for q in range(7)], target)
        sums = force_and_jerk(sums)
        for q in range(6):
            line = jnp.sum(sums[q], axis=1, keepdims=True)
            total = jnp.where(lane == 64 * (g % 2) + CAP * q + g // 2, total + line, total)
    if step == STEPS - 1:
        upper = back(total, 64)
        for r in range(CAP):
            sums_out[r] = total[r : r + 1]
            sums_out[CAP + r] = upper[r : r + 1]
    else:
        sums_out[...] = jnp.broadcast_to(total[None], sums_out.shape)


def correct(old_acc, old_jerk, new_acc, new_jerk, interval):
    diff = old_acc - new_acc
    interval_sq = interval * interval
    second = (-6.0 * diff - interval * (4.0 * old_jerk + 2.0 * new_jerk)) / interval_sq
    third = (12.0 * diff + 6.0 * interval * (old_jerk + new_jerk)) / (interval_sq * interval)
    pos_step = interval_sq * interval_sq * (second / 24.0 + interval * third / 120.0)
    vel_step = interval_sq * interval * (second / 6.0 + interval * third / 24.0)
    return (pos_step, vel_step)


def add_peers(gathered):
    total = gathered[0]
    for p in range(1, NROW):
        total = total + gathered[p]
    return jnp.concatenate([total, back(total, 64)], axis=0)


def correct_rows(step, total, z, names):
    block_time = (step + 1) * step_size
    lane = lane_of(z.shape)
    times = back(z, 96)
    held_at = jnp.maximum(times, step_size)
    held_acc, old_jerk = back(z, 48), back(z, 72)
    x, v = predict(z, back(z, 24), held_acc, old_jerk, block_time - held_at)
    old_acc = held_acc - (held_at - times) * old_jerk
    tau = block_time - times
    new_a, new_j = total, back(total, 24)
    pos_step, vel_step = correct(old_acc, old_jerk, new_a, new_j, tau)

    def lay(*parts):
        out = parts[-1]
        for n in reversed(range(len(parts) - 1)):
            piece = pltpu.roll(parts[n], 24 * n, 1) if n else parts[n]
            out = jnp.where(lane < 24 * (n + 1), piece, out)
        return out

    filled = names < float(STARS)
    rest = jnp.where(lane < 120, block_time, z)
    corrected = lay(x + pos_step, v + vel_step, new_a, new_j, rest)
    terms = lay(new_a, new_j, pos_step, vel_step, jnp.zeros_like(z))
    return jnp.where(filled, corrected, 0.0), jnp.where(filled, terms, 0.0)


def correct_kernel(step, me_of, *refs):
    gathered, target_rows, *refs = refs
    targets = None
    if step > 0:
        targets, *refs = refs
    corrected_out, fresh_out, terms_out, keep = refs
    me = me_of()
    z = target_rows_at(target_rows, 0) if step == 0 else targets[...]
    names = target_rows_at(target_rows, STEPS + step)
    corrected, terms = correct_rows(step, add_peers(gathered), z, names)
    lane = lane_of((NROW, LANES))
    keep[0] = terms
    terms_out[...] = keep[0, pl.ds(me, 1), :]
    keep[1] = jnp.where((lane >= 104) & (lane < 112), names, corrected)
    fresh_out[...] = jnp.broadcast_to(keep[1, pl.ds(me, 1), :][None], fresh_out.shape)
    corrected_out[...] = corrected


def spread(line):
    diagonal = lane_of((16, LANES)) // CAP == row_of((16, LANES))
    x = jnp.where(diagonal, jnp.broadcast_to(line, (16, LANES)), 0.0)
    for shift in (64, 32, 16, 8):
        x = x + pltpu.roll(x, shift, 1)
    return x


def put(whole, names, line):
    columns = spread(line)
    star = lane_of((16, STARS)).astype(jnp.float32)
    for s in range(CAP):
        whole = jnp.where(star == names[:, s : s + 1], columns[:, s : s + 1], whole)
    return whole


def slot_terms(line):
    return jnp.transpose(spread(line))[0:CAP, 0:12]


def last_kernel(me_of, *refs):
    gathered, target_rows, targets, state = refs[:4]
    corrected, terms = refs[4 : STEPS + 3], refs[STEPS + 3 : 2 * STEPS + 2]
    new_pos, new_vel, new_acc, new_jerk, terms_out = refs[2 * STEPS + 2 :]
    me = me_of()
    names = [target_rows[pl.ds(CAP * me + STEPS + j, 1), :] for j in range(STEPS)]
    total = jnp.sum(gathered[...], axis=0, keepdims=True)
    own, own_terms = correct_rows(STEPS - 1, total, targets[pl.ds(me, 1), :], names[-1])
    whole = state[...]
    for j in range(STEPS):
        last = j == STEPS - 1
        whole = put(whole, names[j], own if last else corrected[j][pl.ds(me, 1), :])
        terms_out[j] = slot_terms(own_terms if last else terms[j][...])
    for n, out in enumerate((new_pos, new_vel, new_acc, new_jerk)):
        out[...] = whole[3 * n : 3 * n + 3, :]


def struct(*shape):
    return jax.ShapeDtypeStruct(shape, jnp.float32)


def scratch(*shape):
    return pltpu.VMEM(shape, jnp.float32)


vmem = pl.BlockSpec(memory_space=pltpu.VMEM)
hbm = pl.BlockSpec(memory_space=pltpu.HBM)
smem = pl.BlockSpec(memory_space=pltpu.SMEM)
anywhere = pl.BlockSpec(memory_space=pl.ANY)


def call(kernel, operands, outs, work, specs=None, out_specs=None, flops=None):
    cost = None
    if flops:
        cost = pl.CostEstimate(flops=flops, bytes_accessed=1 << 20, transcendentals=0)
    return pl.pallas_call(
        kernel,
        out_shape=tuple(outs),
        in_specs=specs or [vmem] * len(operands),
        out_specs=out_specs or (vmem,) * len(outs),
        scratch_shapes=work,
        cost_estimate=cost,
        compiler_params=pltpu.CompilerParams(vmem_limit_bytes=8 << 20),
    )(*operands)


def send_all(x, axes):
    return lax.all_to_all(x, axes, split_axis=0, concat_axis=0, tiled=True)


def body(sizes, row_axes, col_axes, pos, vel, acc, jerk, masses, levels, active):
    masses, levels = masses.reshape(1, STARS), levels.reshape(1, STARS)
    pos, vel, acc, jerk, masses, levels, active = (
        pltpu.with_memory_space_constraint(a, pltpu.HBM)
        for a in (pos, vel, acc, jerk, masses, levels, active)
    )
    ncol = math.prod(sizes[axis] for axis in col_axes)

    def me_of():
        me = 0
        for axis in row_axes:
            me = me * sizes[axis] + lax.axis_index(axis)
        return me

    block, rows, state = call(
        pack_kernel,
        (pos, vel, acc, jerk, masses, levels, active),
        (struct(ncol * BLOCK, LANES), struct(NROW, 8, LANES), struct(16, STARS)),
        [scratch(3, STARS)] * 4
        + [scratch(1, STARS), pltpu.VMEM((1, STARS), jnp.int32)]
        + [pltpu.SMEM((STEPS, CAP), jnp.int32)]
        + [scratch(16, STARS), scratch(32, LANES), scratch(8, LANES)]
        + [pltpu.SemaphoreType.DMA((7,))],
        [hbm] * 7,
    )
    target_rows = send_all(rows, row_axes).reshape(NROW * 8, LANES)
    block, target_rows = lax.optimization_barrier((block, target_rows))
    block = block.reshape(ncol, 1, BLOCK * LANES)
    raw = send_all(block, col_axes).reshape(ncol * BLOCK, LANES)

    sums_shape = struct(NROW, NROW // 2, LANES)
    source_shape = (7, 2 * ncol, LANES)
    slots = struct(NROW, LANES)
    splat_shape = (6 * TARGETS, LANES)
    plan_work = [
        pltpu.VMEM((8, LANES), jnp.int32),
        pltpu.SMEM((8, LANES), jnp.int32),
        pltpu.SemaphoreType.DMA,
        pltpu.SMEM((LIST,), jnp.int32),
    ]
    source_work, splat_work = scratch(*source_shape), scratch(*splat_shape)
    (sums,) = call(
        functools.partial(first_force_kernel, ncol),
        (raw, target_rows),
        (sums_shape,),
        [*plan_work, source_work, splat_work, splat_work],
    )
    corrected, terms = [], []
    targets = columns = None
    for step in range(STEPS):
        gathered = send_all(sums, row_axes)
        if step == STEPS - 1:
            break
        operands = [gathered, target_rows] + ([] if step == 0 else [targets])
        done, fresh, own_terms = call(
            functools.partial(correct_kernel, step, me_of),
            operands,
            (slots, struct(ncol, 1, LANES), struct(1, LANES)),
            [scratch(2, NROW, LANES)],
        )
        corrected.append(done)
        terms.append(own_terms)
        fresh = send_all(fresh, col_axes).reshape(ncol, LANES)
        static, splat, targets = call(
            functools.partial(static_kernel, step + 1, ncol),
            (raw, target_rows, *corrected),
            (struct(8, LANES), struct(*splat_shape), slots),
            [*plan_work, source_work, splat_work],
            flops=3 * 10**7,
        )
        blocks = max(ncol // 16, 1) * (step + 1)
        operands = [static, splat, fresh] + ([] if step == 0 else [columns])
        outs, work = [sums_shape], [scratch(7, blocks, LANES)]
        if step + 1 < STEPS - 1:
            outs.append(struct(16 * blocks, LANES))
        else:
            outs[0] = struct(NROW, 1, LANES)
            work.insert(0, scratch(16 * blocks, LANES))
        sums, *columns = call(
            functools.partial(fresh_kernel, step + 1, ncol), operands, outs, work
        )
        if columns:
            (columns,) = columns
    *new, slot_rows = call(
        functools.partial(last_kernel, me_of),
        (gathered.reshape(NROW, LANES), target_rows, targets, state, *corrected, *terms),
        (struct(3, STARS),) * 4 + (struct(STEPS, CAP, 12),),
        [],
    )
    return (*new, jnp.swapaxes(slot_rows, 1, 2))


def solution(mesh):
    sizes = {"x": 4, "z": mesh.shape["wide"] // 8, "core": 2, "narrow": mesh.shape["narrow"]}
    row_axes, col_axes = ("core", "narrow"), ("z", "x")
    every = tuple(sizes)
    finer = Mesh(mesh.devices.reshape(tuple(sizes.values())), every)
    in_specs = (P(None, every),) * 4 + (P(every), P(every), P(None, every))
    out_specs = (P(None, every),) * 4 + (P(None, None, every),)
    return jax.shard_map(
        functools.partial(body, sizes, row_axes, col_axes),
        mesh=finer,
        in_specs=in_specs,
        out_specs=out_specs,
        check_vma=False,
    )
```
